32 devices in a mesh: branch: 4 (over y, core), leaf: 8 (over z, x).
Axes of the slice: x: 2, y: 2, z: 4, core: 2. Of those that a mesh axis runs over, the one named last changes fastest.
Arguments:
- values: bfloat16 [2, 16, 16384], P(None, None, ('branch', 'leaf')), may hold values from -6 to 6
- leaf_basis: bfloat16 [256, 64, 64], P(('branch', 'leaf')), may hold values from -0.75 to 0.75
- transfer: bfloat16 [448, 64, 64], P(('branch', 'leaf')), may hold values from -0.625 to 0.625
- local_coupling: bfloat16 [2, 448, 12, 64, 64], P(None, ('branch', 'leaf')), may hold values from -0.21875 to 0.21875
- coupling_source: int32 [448, 12], P(('branch', 'leaf')), may hold values from 0 to 23, as said below
- near_field: bfloat16 [2, 256, 12, 64, 64], P(None, ('branch', 'leaf')), may hold values from -0.21875 to 0.21875
- near_source: int32 [256, 12], P(('branch', 'leaf')), may hold values from 0 to 23, as said below
- upper_transfer: bfloat16 [4, 14, 64, 64], P('branch'), may hold values from -0.625 to 0.625
- upper_coupling: bfloat16 [2, 4, 14, 64, 64], P(None, 'branch'), may hold values from -0.75 to 0.75
- top_coupling: bfloat16 [2, 4, 3, 64, 64], P(None, 'branch'), may hold values from -0.4375 to 0.4375
Outputs:
- result: float32 [2, 16, 16384], P(None, None, ('branch', 'leaf'))
The draws below stay inside these ranges and needn't reach their ends.
Inputs may be any that keep to these rules, and one draw needn't show every extreme that they name: `coupling_source`: entry of row r(l, p, t) lies in t to t + 2 * n_l, so its source is within n_l clusters of the target along the device order. `near_source`: entry of leaf t of a device lies in t to t + 16, so its source leaf is within 8 leaves of the target.
All inputs are finite; a program needn't handle non-finite values.
Results may differ from the reference program's by a relative error of at most 0.027.
Values may be sent and summed in bfloat16 or wider, within the bound.
A program may use at most 64 MiB of HBM per device.

```python
import jax
import jax.numpy as jnp
from jax import lax

R = 64
LS = 64
RHS = 16
LOG_LEAF = 3
CPL = 12
NEAR = 12
LEAF_DEV = 8
NLEAF = 256
POINTS = 16384
CROWS = 448
UPPER = 14
N_BRANCH = 4
N_LEAF = 8


def draw_coupling_source(key, part):
    key = jax.random.fold_in(key, 11)
    rows = 2 * LEAF_DEV - 2
    local = jnp.arange(CROWS, dtype=jnp.int32) % rows
    count = jnp.zeros((CROWS,), jnp.int32)
    position = jnp.zeros((CROWS,), jnp.int32)
    for level in range(LOG_LEAF):
        size_here = LEAF_DEV >> level
        begin = 2 * LEAF_DEV - 2 * size_here
        inside = (local >= begin) & (local < begin + size_here)
        count = jnp.where(inside, size_here, count)
        position = jnp.where(inside, local - begin, position)
    lower = position[:, None]
    upper = (position + 2 * count + 1)[:, None]
    return jax.random.randint(key, (CROWS, CPL), lower, upper, dtype=jnp.int32)


def draw_near_source(key, part):
    key = jax.random.fold_in(key, 23)
    position = jnp.arange(NLEAF, dtype=jnp.int32) % LEAF_DEV
    lower = position[:, None]
    upper = (position + 2 * LEAF_DEV + 1)[:, None]
    return jax.random.randint(key, (NLEAF, NEAR), lower, upper, dtype=jnp.int32)


def level_of(key, dims, pieces, low, top_value):
    factor_of, own = 1.0, jax.random.fold_in(key, 6)
    for dim, shards_of in pieces:
        steps = jnp.exp(jax.random.uniform(jax.random.fold_in(own, dim), (shards_of,), jnp.float32, low / len(pieces), top_value / len(pieces)))
        factor_of = factor_of * jnp.repeat(steps, dims[dim] // shards_of).reshape([-1 if axis == dim else 1 for axis in range(len(dims))])
    return factor_of


def bell_draw(own_key, extent, width, most, cuts=(), kind=jnp.bfloat16):
    entries = width * jax.random.normal(own_key, extent, jnp.float32)
    if cuts:
        entries = entries * level_of(own_key, extent, cuts, -0.22, 0.18)
    return jnp.clip(entries, -most, most).astype(kind)


def setup_inputs(seed: int = 0) -> dict:
    splits = jax.random.split(jax.random.key(seed), 11)
    values = bell_draw(splits[0], (2, RHS, POINTS), 1.0, 6.0, ((2, 32),))
    leaf_basis = bell_draw(splits[1], (NLEAF, LS, R), LS ** -0.5, 0.75, ((0, 32),))
    transfer = bell_draw(splits[2], (CROWS, R, R), (3 * R // 2) ** -0.5, 0.625, ((0, 32),))
    local_coupling = bell_draw(splits[3], (2, CROWS, CPL, R, R), (CPL * R) ** -0.5, 0.21875, ((1, 32),))
    coupling_source = draw_coupling_source(jax.random.fold_in(splits[10], 71), 0)
    near_field = bell_draw(splits[5], (2, NLEAF, NEAR, LS, LS), (NEAR * LS) ** -0.5, 0.21875, ((1, 32),))
    near_source = draw_near_source(jax.random.fold_in(splits[10], 71), 0)
    upper_transfer = bell_draw(splits[7], (N_BRANCH, UPPER, R, R), (3 * R // 2) ** -0.5, 0.625, ((0, 4),))
    upper_coupling = bell_draw(splits[8], (2, N_BRANCH, UPPER, R, R), R ** -0.5, 0.75, ((1, 4),))
    top_coupling = bell_draw(splits[9], (2, N_BRANCH, N_BRANCH - 1, R, R), ((N_BRANCH - 1) * R) ** -0.5, 0.4375, ((1, 4),))
    return dict(values=values, leaf_basis=leaf_basis, transfer=transfer, local_coupling=local_coupling, coupling_source=coupling_source, near_field=near_field, near_source=near_source, upper_transfer=upper_transfer, upper_coupling=upper_coupling, top_coupling=top_coupling)


def window(blocks):
    zero = jnp.zeros_like(blocks[:1])
    before = jnp.concatenate([zero, blocks[:-1]], axis=0)
    after = jnp.concatenate([blocks[1:], zero], axis=0)
    return jnp.stack([before, blocks, after], axis=1)


def reference(values, leaf_basis, transfer, local_coupling, coupling_source, near_field, near_source, upper_transfer, upper_coupling, top_coupling):
    f32 = jnp.float32
    bf16 = jnp.bfloat16
    devs = N_BRANCH * N_LEAF
    rows = 2 * LEAF_DEV - 2
    xv = values.reshape(2, RHS, devs, LEAF_DEV, LS)
    basis = leaf_basis.reshape(devs, LEAF_DEV, LS, R)
    trans = transfer.reshape(devs, rows, R, R)
    coef = jnp.einsum('grplq,plqk->plgrk', xv.astype(f32), basis.astype(f32)).astype(bf16)
    levels = [coef]
    begin = 0
    for level in range(1, LOG_LEAF + 1):
        count = LEAF_DEV >> (level - 1)
        part = jnp.einsum('pcgrk,pckm->pcgrm', levels[-1].astype(f32), trans[:, begin:begin + count].astype(f32))
        part = part.reshape(devs, count // 2, 2, 2, RHS, R)
        levels.append((part[:, :, 0] + part[:, :, 1]).astype(bf16))
        begin += count
    roots = levels[-1][:, 0]
    depth = N_LEAF.bit_length() - 1
    current = roots.reshape(N_BRANCH, N_LEAF, 2, RHS, R)
    uppers = [current]
    offsets = []
    for step in range(1, depth + 1):
        count = N_LEAF >> (step - 1)
        offset = 2 * N_LEAF - 2 * count
        offsets.append(offset)
        part = jnp.einsum('bjgrk,bjkm->bjgrm', current.astype(f32), upper_transfer[:, offset:offset + count].astype(f32))
        part = part.reshape(N_BRANCH, count // 2, 2, 2, RHS, R)
        current = (part[:, :, 0] + part[:, :, 1]).astype(bf16)
        uppers.append(current)
    subtree_roots = current[:, 0]
    order = (jnp.arange(N_BRANCH, dtype=jnp.int32)[:, None] + 1 + jnp.arange(N_BRANCH - 1, dtype=jnp.int32)[None, :]) % N_BRANCH
    others = subtree_roots[order]
    down = jnp.einsum('bjgrm,gbjkm->bgrk', others.astype(f32), top_coupling.astype(f32)).astype(bf16)[:, None]
    for step in range(depth, 0, -1):
        count = N_LEAF >> (step - 1)
        offset = offsets[step - 1]
        child = uppers[step - 1]
        sibling = child.reshape(N_BRANCH, count // 2, 2, 2, RHS, R)[:, :, ::-1].reshape(N_BRANCH, count, 2, RHS, R)
        coupled = jnp.einsum('bjgrm,gbjkm->bjgrk', sibling.astype(f32), upper_coupling[:, :, offset:offset + count].astype(f32))
        parent = jnp.repeat(down, 2, axis=1)
        carried = jnp.einsum('bjgrm,bjkm->bjgrk', parent.astype(f32), upper_transfer[:, offset:offset + count].astype(f32))
        down = (coupled + carried).astype(bf16)
    device_roots = down.reshape(devs, 2, RHS, R)
    stack = jnp.concatenate(levels[:LOG_LEAF], axis=1)
    coef_window = window(stack)
    value_window = window(jnp.moveaxis(xv, 2, 0))
    coupling_all = local_coupling.reshape(2, devs, rows, CPL, R, R)
    sources_all = coupling_source.reshape(devs, rows, CPL)
    near_all = near_field.reshape(2, devs, LEAF_DEV, NEAR, LS, LS)
    near_src_all = near_source.reshape(devs, LEAF_DEV, NEAR)

    def per_device(index):
        win = lax.dynamic_index_in_dim(coef_window, index, 0, keepdims=False)
        couple = lax.dynamic_index_in_dim(coupling_all, index, 1, keepdims=False)
        sources = lax.dynamic_index_in_dim(sources_all, index, 0, keepdims=False)
        mats = lax.dynamic_index_in_dim(trans, index, 0, keepdims=False)
        parent = lax.dynamic_index_in_dim(device_roots, index, 0, keepdims=True)
        for level in range(LOG_LEAF - 1, -1, -1):
            count = LEAF_DEV >> level
            start = 2 * LEAF_DEV - 2 * count
            rows_win = win[:, start:start + count].reshape(3 * count, 2, RHS, R)
            picked = rows_win[sources[start:start + count]]
            coupled = jnp.einsum('cjgrm,gcjkm->cgrk', picked.astype(f32), couple[:, start:start + count].astype(f32))
            carried = jnp.einsum('cgrm,ckm->cgrk', jnp.repeat(parent, 2, axis=0).astype(f32), mats[start:start + count].astype(f32))
            parent = (coupled + carried).astype(bf16)
        own_basis = lax.dynamic_index_in_dim(basis, index, 0, keepdims=False)
        far = jnp.einsum('lgrk,lqk->grlq', parent.astype(f32), own_basis.astype(f32))
        xw = lax.dynamic_index_in_dim(value_window, index, 0, keepdims=False)
        cells = jnp.transpose(xw, (1, 2, 0, 3, 4)).reshape(2, RHS, 3 * LEAF_DEV, LS)
        near_src = lax.dynamic_index_in_dim(near_src_all, index, 0, keepdims=False)
        picked_cells = cells[:, :, near_src]
        blocks = lax.dynamic_index_in_dim(near_all, index, 1, keepdims=False)
        near = jnp.einsum('grljq,gljpq->grlp', picked_cells.astype(f32), blocks.astype(f32))
        return (far + near).reshape(2, RHS, LEAF_DEV * LS)

    outputs = lax.map(per_device, jnp.arange(devs, dtype=jnp.int32))
    return jnp.transpose(outputs, (1, 2, 0, 3)).reshape(2, RHS, devs * LEAF_DEV * LS)
```

```python
import functools

import jax
import jax.numpy as jnp
from jax import lax
from jax.experimental import pallas as pl
from jax.experimental.pallas import tpu as pltpu
from jax.sharding import PartitionSpec as P

LOG_LEAF = 3
F32 = jnp.float32
BF16 = jnp.bfloat16
MESH = pl.DeviceIdType.MESH


def dot(a, b):
    return jnp.dot(a, b, preferred_element_type=F32)


def dot_nt(a, b):
    return lax.dot_general(a, b, (((1,), (1,)), ((), ())), preferred_element_type=F32)


def side_by_side(blocks):
    pairs = []
    for i in range(0, len(blocks) - 1, 2):
        pairs.append(jnp.concatenate(blocks[i : i + 2], axis=1))
    if len(blocks) % 2:
        pairs.append(blocks[-1])
    return pairs[0] if len(pairs) == 1 else jnp.concatenate(pairs, axis=1)


def kernel(
    branch_count,
    leaf_count,
    values,
    leaf_basis,
    transfer,
    local_coupling,
    near_field,
    upper_transfer,
    upper_coupling,
    top_coupling,
    coupling_source,
    near_source,
    out,
    val,
    basis,
    trans,
    couple,
    near,
    up_trans,
    up_couple,
    top,
    value_win,
    coef_win,
    upper,
    roots,
    coupled,
    near_part,
    load_sem,
    halo_send,
    halo_recv,
    leaf_send,
    leaf_recv,
    branch_send,
    branch_recv,
):
    operators, rhs_count, _ = val.shape
    cols = operators * rhs_count
    leaves, leaf_size, rank = basis.shape
    rows = trans.shape[0]
    blocks = couple.shape[2]
    near_blocks = near.shape[2]
    depth = leaf_count.bit_length() - 1
    b = lax.axis_index("branch")
    j = lax.axis_index("leaf")
    p = b * leaf_count + j
    last = branch_count * leaf_count - 1

    starts = [2 * leaves - 2 * (leaves >> level) for level in range(LOG_LEAF)]
    pieces = [
        (values, val),
        (leaf_basis, basis),
        (transfer, trans),
        (upper_transfer.at[0], up_trans),
        (near_field, near),
        (local_coupling, couple),
        (upper_coupling.at[:, 0], up_couple),
        (top_coupling.at[:, 0], top),
    ]
    loads = [
        pltpu.make_async_copy(src, dst, load_sem.at[i]) for i, (src, dst) in enumerate(pieces)
    ]
    for load in loads:
        load.start()
    val_load, basis_load, trans_load, ut_load, near_load, couple_load, uc_load, top_load = loads

    barrier = pltpu.get_barrier_semaphore()

    def greet(bb, jj):
        pl.semaphore_signal(barrier, inc=1, device_id=(bb, jj), device_id_type=MESH)

    for d in range(1, leaf_count):
        greet(b, lax.rem(j + d, leaf_count))
    for d in range(1, branch_count):
        greet(lax.rem(b + d, branch_count), j)
    low_edge = jnp.logical_and(j == 0, b > 0)
    high_edge = jnp.logical_and(j == leaf_count - 1, b < branch_count - 1)

    @pl.when(low_edge)
    def _():
        greet(b - 1, leaf_count - 1)

    @pl.when(high_edge)
    def _():
        greet(b + 1, 0)

    @pl.when(p == 0)
    def _():
        value_win[0:leaves] = jnp.zeros((leaves, cols, leaf_size), BF16)
        coef_win[0:rows] = jnp.zeros((rows, cols, rank), BF16)

    @pl.when(p == last)
    def _():
        value_win[2 * leaves :] = jnp.zeros((leaves, cols, leaf_size), BF16)
        coef_win[2 * rows :] = jnp.zeros((rows, cols, rank), BF16)

    val_load.wait()
    basis_load.wait()
    cells = val[...].reshape(cols, leaves * leaf_size)
    level = []
    for t in range(leaves):
        cell = cells[:, t * leaf_size : (t + 1) * leaf_size]
        value_win[leaves + t] = cell
        coef = dot(cell, basis[t]).astype(BF16)
        coef_win[rows + t] = coef
        level.append(coef)
    trans_load.wait()
    begin = 0
    for step in range(LOG_LEAF):
        count = leaves >> step
        above = []
        for t in range(count // 2):
            pair = side_by_side(level[2 * t : 2 * t + 2])
            mats = trans[begin + 2 * t : begin + 2 * t + 2].reshape(2 * rank, rank)
            coef = dot(pair, mats).astype(BF16)
            if step < LOG_LEAF - 1:
                coef_win[rows + begin + count + t] = coef
            above.append(coef)
        begin += count
        level = above
    upper[j] = level[0]

    greeted = leaf_count - 1 + branch_count - 1
    greeted += low_edge.astype(jnp.int32) + high_edge.astype(jnp.int32)
    pl.semaphore_wait(barrier, greeted)

    def leaf_copy(d, slot):
        return pltpu.make_async_remote_copy(
            src_ref=upper.at[slot],
            dst_ref=upper.at[slot],
            send_sem=leaf_send.at[d - 1],
            recv_sem=leaf_recv.at[d - 1],
            device_id=(b, lax.rem(j + d, leaf_count)),
            device_id_type=MESH,
        )

    for d in range(1, leaf_count):
        leaf_copy(d, j).start()

    def halo(window, size, kind, way):
        place = 0 if way == 0 else 2 * size
        other = p + 1 if way == 0 else p - 1
        return pltpu.make_async_remote_copy(
            src_ref=window.at[pl.ds(size, size)],
            dst_ref=window.at[pl.ds(place, size)],
            send_sem=halo_send.at[2 * kind + way],
            recv_sem=halo_recv.at[2 * kind + way],
            device_id=(other // leaf_count, lax.rem(other, leaf_count)),
            device_id_type=MESH,
        )

    halos = ((value_win, leaves, 0), (coef_win, rows, 1))

    @pl.when(p < last)
    def _():
        for args in halos:
            halo(*args, 0).start()

    @pl.when(p > 0)
    def _():
        for args in halos:
            halo(*args, 1).start()

    ut_load.wait()
    for d in range(1, leaf_count):
        leaf_copy(d, lax.rem(j + leaf_count - d, leaf_count)).wait_recv()
    offsets = [2 * leaf_count - 2 * (leaf_count >> step) for step in range(depth + 1)]
    for step in range(depth):
        for t in range(leaf_count >> step + 1):
            low = offsets[step] + 2 * t
            pair = side_by_side([upper[low], upper[low + 1]])
            mats = up_trans[low : low + 2].reshape(2 * rank, rank)
            upper[offsets[step + 1] + t] = dot(pair, mats).astype(BF16)

    def branch_copy(d):
        return pltpu.make_async_remote_copy(
            src_ref=upper.at[offsets[depth]],
            dst_ref=roots.at[branch_count - 1 - d],
            send_sem=branch_send.at[d - 1],
            recv_sem=branch_recv.at[d - 1],
            device_id=(lax.rem(b + d, branch_count), j),
            device_id_type=MESH,
        )

    for d in range(1, branch_count):
        branch_copy(d).start()

    first = lax.broadcasted_iota(jnp.int32, (rank, cols), 1) < rhs_count

    def pick(both):
        return jnp.where(first, both[:rank], both[rank:])

    near_load.wait()

    @pl.when(p > 0)
    def _():
        halo(value_win, leaves, 0, 0).wait_recv()
        halo(coef_win, rows, 1, 0).wait_recv()

    @pl.when(p < last)
    def _():
        halo(value_win, leaves, 0, 1).wait_recv()
        halo(coef_win, rows, 1, 1).wait_recv()

    def listed(matrices, row, count, window, source):
        wide = side_by_side(
            [matrices[:, row, m].reshape(operators * rank, rank) for m in range(count)]
        )
        picked = side_by_side([window[source(m)] for m in range(count)])
        return pick(dot_nt(wide, picked))

    def near_step(t, carry):
        near_part[t] = listed(near, t, near_blocks, value_win, lambda m: near_source[t, m])
        return carry

    lax.fori_loop(0, leaves, near_step, 0, unroll=2)
    couple_load.wait()

    for step in range(LOG_LEAF):
        count = leaves >> step
        begin = starts[step]

        def couple_step(t, carry, count=count, begin=begin, shift=LOG_LEAF - step):
            row = begin + t

            def source(m):
                s = coupling_source[row, m]
                side = jnp.right_shift(s, shift)
                return side * rows + begin + jnp.bitwise_and(s, count - 1)

            coupled[row] = listed(couple, row, blocks, coef_win, source)
            return carry

        lax.fori_loop(0, count, couple_step, 0, unroll=2)

    uc_load.wait()
    top_load.wait()
    sides = []
    for step in range(depth):
        own = jnp.right_shift(j, step)
        mats = up_couple[:, offsets[step] + own].reshape(operators * rank, rank)
        sibling = upper[offsets[step] + jnp.bitwise_xor(own, 1)]
        sides.append(pick(dot_nt(mats, sibling)))

    for d in range(1, branch_count):
        branch_copy(d).wait_recv()
    tops = side_by_side(
        [top[:, m].reshape(operators * rank, rank) for m in range(branch_count - 1)]
    )
    others = side_by_side([roots[m] for m in range(branch_count - 1)])
    down = pick(dot_nt(tops, others)).astype(BF16)
    for step in range(depth - 1, -1, -1):
        mat = up_trans[offsets[step] + jnp.right_shift(j, step)]
        down = (sides[step] + dot(mat, down)).astype(BF16)
    targets = [down]
    for step in range(LOG_LEAF - 1, -1, -1):
        below = []
        for t, parent in enumerate(targets):
            low = starts[step] + 2 * t
            mats = trans[low : low + 2].reshape(2 * rank, rank)
            both = coupled[low : low + 2].reshape(2 * rank, cols) + dot(mats, parent)
            both = both.astype(BF16)
            below += [both[:rank], both[rank:]]
        targets = below
    for t in range(0, leaves, 2):
        parts = [near_part[u] + dot(basis[u], targets[u]) for u in (t, t + 1)]
        turned = jnp.concatenate(parts, axis=0).T
        out[:, :, t * leaf_size : (t + 2) * leaf_size] = turned.reshape(
            operators, rhs_count, 2 * leaf_size
        )

    for d in range(1, leaf_count):
        leaf_copy(d, j).wait_send()
    for d in range(1, branch_count):
        branch_copy(d).wait_send()

    @pl.when(p < last)
    def _():
        for args in halos:
            halo(*args, 0).wait_send()

    @pl.when(p > 0)
    def _():
        for args in halos:
            halo(*args, 1).wait_send()


def solution(mesh):
    branch_count = mesh.shape["branch"]
    leaf_count = mesh.shape["leaf"]

    def per_device(
        values,
        leaf_basis,
        transfer,
        local_coupling,
        coupling_source,
        near_field,
        near_source,
        upper_transfer,
        upper_coupling,
        top_coupling,
    ):
        operators, rhs_count, width = values.shape
        cols = operators * rhs_count
        leaves, leaf_size, rank = leaf_basis.shape
        rows = transfer.shape[0]
        upper = upper_transfer.shape[1]
        any_spec = pl.BlockSpec(memory_space=pl.ANY)
        smem = pl.BlockSpec(memory_space=pltpu.SMEM)
        dma = pltpu.SemaphoreType.DMA
        return pl.pallas_call(
            functools.partial(kernel, branch_count, leaf_count),
            out_shape=jax.ShapeDtypeStruct(values.shape, F32),
            in_specs=[any_spec] * 8 + [smem] * 2,
            out_specs=pl.BlockSpec(memory_space=pltpu.VMEM),
            scratch_shapes=[
                pltpu.VMEM(values.shape, BF16),
                pltpu.VMEM(leaf_basis.shape, BF16),
                pltpu.VMEM(transfer.shape, BF16),
                pltpu.VMEM(local_coupling.shape, BF16),
                pltpu.VMEM(near_field.shape, BF16),
                pltpu.VMEM(upper_transfer.shape[1:], BF16),
                pltpu.VMEM((operators,) + upper_coupling.shape[2:], BF16),
                pltpu.VMEM((operators,) + top_coupling.shape[2:], BF16),
                pltpu.VMEM((3 * leaves, cols, leaf_size), BF16),
                pltpu.VMEM((3 * rows, cols, rank), BF16),
                pltpu.VMEM((upper + 1, cols, rank), BF16),
                pltpu.VMEM((branch_count - 1, cols, rank), BF16),
                pltpu.VMEM((rows, rank, cols), F32),
                pltpu.VMEM((leaves, leaf_size, cols), F32),
                dma((8,)),
                dma((4,)),
                dma((4,)),
                dma((leaf_count - 1,)),
                dma((leaf_count - 1,)),
                dma((branch_count - 1,)),
                dma((branch_count - 1,)),
            ],
            compiler_params=pltpu.CompilerParams(
                collective_id=0, has_side_effects=True, vmem_limit_bytes=64 * 1024 * 1024
            ),
        )(
            values,
            leaf_basis,
            transfer,
            local_coupling,
            near_field,
            upper_transfer,
            upper_coupling,
            top_coupling,
            coupling_source,
            near_source,
        )

    in_specs = (
        P(None, None, ("branch", "leaf")),
        P(("branch", "leaf"), None, None),
        P(("branch", "leaf"), None, None),
        P(None, ("branch", "leaf"), None, None, None),
        P(("branch", "leaf"), None),
        P(None, ("branch", "leaf"), None, None, None),
        P(("branch", "leaf"), None),
        P("branch", None, None, None),
        P(None, "branch", None, None, None),
        P(None, "branch", None, None, None),
    )
    out_specs = P(None, None, ("branch", "leaf"))
    return jax.shard_map(
        per_device, mesh=mesh, in_specs=in_specs, out_specs=out_specs, check_vma=False
    )
```

```python
import functools

import jax
import jax.numpy as jnp
from jax import lax
from jax.experimental import pallas as pl
from jax.experimental.pallas import tpu as pltpu
from jax.sharding import PartitionSpec as P

LOG_LEAF = 3
F32 = jnp.float32
BF16 = jnp.bfloat16
MESH = pl.DeviceIdType.MESH


def dot(a, b):
    return jnp.dot(a, b, preferred_element_type=F32)


def dot_nt(a, b):
    return lax.dot_general(a, b, (((1,), (1,)), ((), ())), preferred_element_type=F32)


def side_by_side(blocks):
    pairs = []
    for i in range(0, len(blocks) - 1, 2):
        pairs.append(jnp.concatenate(blocks[i : i + 2], axis=1))
    if len(blocks) % 2:
        pairs.append(blocks[-1])
    return pairs[0] if len(pairs) == 1 else jnp.concatenate(pairs, axis=1)


def kernel(
    branch_count,
    leaf_count,
    values,
    leaf_basis,
    transfer,
    local_coupling,
    near_field,
    upper_transfer,
    upper_coupling,
    top_coupling,
    coupling_source,
    near_source,
    out,
    coupling_index,
    near_index,
    val,
    basis,
    trans,
    couple,
    near,
    up_trans,
    up_couple,
    top,
    value_win,
    coef_win,
    leaf_roots,
    upper,
    own_root,
    roots,
    coupled,
    near_part,
    load_sem,
    halo_send,
    halo_recv,
    leaf_send,
    leaf_recv,
    branch_send,
    branch_recv,
):
    operators, rhs_count, _ = val.shape
    cols = operators * rhs_count
    leaves, leaf_size, rank = basis.shape
    rows = trans.shape[0]
    cell_pairs, coef_pairs = leaves // 2, rows // 2
    blocks = couple.shape[2]
    near_blocks = near.shape[2]
    depth = leaf_count.bit_length() - 1
    b = lax.axis_index("branch")
    j = lax.axis_index("leaf")
    p = b * leaf_count + j
    last = branch_count * leaf_count - 1

    starts = [2 * leaves - 2 * (leaves >> level) for level in range(LOG_LEAF)]

    def dense(coef):
        return jnp.concatenate([coef[:rhs_count], coef[rhs_count:]], axis=1)

    def undense(coef):
        return jnp.concatenate([coef[:, :rank], coef[:, rank:]], axis=0)

    pieces = [
        (values, val),
        (leaf_basis, basis),
        (transfer, trans),
        (upper_transfer.at[0], up_trans),
        (near_field, near),
        (local_coupling, couple),
        (upper_coupling.at[:, 0], up_couple),
        (top_coupling.at[:, 0], top),
        (near_source, near_index),
        (coupling_source, coupling_index),
    ]
    loads = [
        pltpu.make_async_copy(src, dst, load_sem.at[i]) for i, (src, dst) in enumerate(pieces)
    ]
    for load in loads:
        load.start()
    val_load, basis_load, trans_load, ut_load, near_load, couple_load, uc_load, top_load, ni_load, ci_load = loads

    barrier = pltpu.get_barrier_semaphore()

    def greet(bb, jj):
        pl.semaphore_signal(barrier, inc=1, device_id=(bb, jj), device_id_type=MESH)

    for d in range(1, leaf_count):
        greet(b, lax.rem(j + d, leaf_count))
    for d in range(1, branch_count):
        greet(lax.rem(b + d, branch_count), j)
    low_edge = jnp.logical_and(j == 0, b > 0)
    high_edge = jnp.logical_and(j == leaf_count - 1, b < branch_count - 1)

    @pl.when(low_edge)
    def _():
        greet(b - 1, leaf_count - 1)

    @pl.when(high_edge)
    def _():
        greet(b + 1, 0)

    @pl.when(p == 0)
    def _():
        value_win[0:cell_pairs] = jnp.zeros((cell_pairs, cols, 2 * leaf_size), BF16)
        coef_win[0:coef_pairs] = jnp.zeros((coef_pairs, cols, 2 * rank), BF16)

    @pl.when(p == last)
    def _():
        value_win[2 * cell_pairs : 3 * cell_pairs] = jnp.zeros(
            (cell_pairs, cols, 2 * leaf_size), BF16
        )
        coef_win[2 * coef_pairs : 3 * coef_pairs] = jnp.zeros((coef_pairs, cols, 2 * rank), BF16)

    val_load.wait()
    basis_load.wait()
    cells = val[...].reshape(cols, leaves * leaf_size)
    level = []
    for t in range(cell_pairs):
        pair = cells[:, 2 * t * leaf_size : 2 * (t + 1) * leaf_size]
        value_win[cell_pairs + t] = pair
        level.append(dot(pair[:, :leaf_size], basis[2 * t]).astype(BF16))
        level.append(dot(pair[:, leaf_size:], basis[2 * t + 1]).astype(BF16))
    trans_load.wait()
    for step in range(LOG_LEAF):
        above = []
        for t in range(leaves >> step + 1):
            low = starts[step] + 2 * t
            pair = side_by_side(level[2 * t : 2 * t + 2])
            coef_win[coef_pairs + low // 2] = pair
            mats = trans[low : low + 2].reshape(2 * rank, rank)
            above.append(dot(pair, mats).astype(BF16))
        level = above
    leaf_roots[j] = dense(level[0])

    greeted = leaf_count - 1 + branch_count - 1
    greeted += low_edge.astype(jnp.int32) + high_edge.astype(jnp.int32)
    pl.semaphore_wait(barrier, greeted)

    def leaf_copy(d, slot):
        return pltpu.make_async_remote_copy(
            src_ref=leaf_roots.at[slot],
            dst_ref=leaf_roots.at[slot],
            send_sem=leaf_send.at[d - 1],
            recv_sem=leaf_recv.at[d - 1],
            device_id=(b, lax.rem(j + d, leaf_count)),
            device_id_type=MESH,
        )

    for d in range(1, leaf_count):
        leaf_copy(d, j).start()

    def halo(window, size, kind, way):
        place = 0 if way == 0 else 2 * size
        other = p + 1 if way == 0 else p - 1
        return pltpu.make_async_remote_copy(
            src_ref=window.at[pl.ds(size, size)],
            dst_ref=window.at[pl.ds(place, size)],
            send_sem=halo_send.at[2 * kind + way],
            recv_sem=halo_recv.at[2 * kind + way],
            device_id=(other // leaf_count, lax.rem(other, leaf_count)),
            device_id_type=MESH,
        )

    halos = ((value_win, cell_pairs, 0), (coef_win, coef_pairs, 1))

    @pl.when(p < last)
    def _():
        for args in halos:
            halo(*args, 0).start()

    @pl.when(p > 0)
    def _():
        for args in halos:
            halo(*args, 1).start()

    ut_load.wait()
    for d in range(1, leaf_count):
        leaf_copy(d, lax.rem(j + leaf_count - d, leaf_count)).wait_recv()
    offsets = [2 * leaf_count - 2 * (leaf_count >> step) for step in range(depth + 1)]
    level = [undense(leaf_roots[m]) for m in range(leaf_count)]
    for step in range(depth):
        above = []
        for t in range(leaf_count >> step + 1):
            low = offsets[step] + 2 * t
            pair = side_by_side(level[2 * t : 2 * t + 2])
            mats = up_trans[low : low + 2].reshape(2 * rank, rank)
            coef = dot(pair, mats).astype(BF16)
            if step < depth - 1:
                upper[offsets[step + 1] - leaf_count + t] = coef
            above.append(coef)
        level = above
    own_root[...] = dense(level[0])

    def branch_copy(d):
        return pltpu.make_async_remote_copy(
            src_ref=own_root,
            dst_ref=roots.at[branch_count - 1 - d],
            send_sem=branch_send.at[d - 1],
            recv_sem=branch_recv.at[d - 1],
            device_id=(lax.rem(b + d, branch_count), j),
            device_id_type=MESH,
        )

    for d in range(1, branch_count):
        branch_copy(d).start()

    first = lax.broadcasted_iota(jnp.int32, (rank, cols), 1) < rhs_count

    def pick(both):
        return jnp.where(first, both[:rank], both[rank:])

    near_load.wait()

    @pl.when(p > 0)
    def _():
        for args in halos:
            halo(*args, 0).wait_recv()

    @pl.when(p < last)
    def _():
        for args in halos:
            halo(*args, 1).wait_recv()

    for window, size, _ in halos:
        for m in range(3 * size):
            pair = window[m]
            half = pair.shape[1] // 2
            window[3 * size + m] = jnp.concatenate([pair[:, half:], pair[:, :half]], axis=1)

    def listed(matrices, row, count, window, source):
        wide = side_by_side(
            [matrices[:, row, m].reshape(operators * rank, rank) for m in range(count)]
        )
        picked = []
        for m in range(0, count, 2):
            half = window.shape[2] // 2
            left, right = window[source(m)], window[source(m + 1)]
            picked.append(jnp.concatenate([left[:, :half], right[:, half:]], axis=1))
        return pick(dot_nt(wide, jnp.concatenate(picked, axis=1)))

    ni_load.wait()

    def near_step(t, carry):
        def source(m):
            s = near_index[t, m]
            return jnp.bitwise_and(s + m, 1) * 3 * cell_pairs + jnp.right_shift(s, 1)

        near_part[t] = listed(near, t, near_blocks, value_win, source)
        return carry

    lax.fori_loop(0, leaves, near_step, 0, unroll=2)
    couple_load.wait()
    ci_load.wait()

    for step in range(LOG_LEAF):
        count = leaves >> step
        begin = starts[step]

        def couple_step(t, carry, count=count, begin=begin, shift=LOG_LEAF - step):
            row = begin + t

            def source(m):
                s = coupling_index[row, m]
                side = jnp.right_shift(s, shift)
                place = jnp.right_shift(jnp.bitwise_and(s, count - 1), 1)
                turned = jnp.bitwise_and(s + m, 1) * 3 * coef_pairs
                return turned + side * coef_pairs + begin // 2 + place

            coupled[row] = listed(couple, row, blocks, coef_win, source)
            return carry

        lax.fori_loop(0, count, couple_step, 0, unroll=2)

    uc_load.wait()
    top_load.wait()
    sides = []
    for step in range(depth):
        own = jnp.right_shift(j, step)
        mats = up_couple[:, offsets[step] + own].reshape(operators * rank, rank)
        sibling = jnp.bitwise_xor(own, 1)
        if step == 0:
            sibling = undense(leaf_roots[sibling])
        else:
            sibling = upper[offsets[step] - leaf_count + sibling]
        sides.append(pick(dot_nt(mats, sibling)))

    for d in range(1, branch_count):
        branch_copy(d).wait_recv()
    tops = side_by_side(
        [top[:, m].reshape(operators * rank, rank) for m in range(branch_count - 1)]
    )
    others = side_by_side([undense(roots[m]) for m in range(branch_count - 1)])
    down = pick(dot_nt(tops, others)).astype(BF16)
    for step in range(depth - 1, -1, -1):
        mat = up_trans[offsets[step] + jnp.right_shift(j, step)]
        down = (sides[step] + dot(mat, down)).astype(BF16)
    targets = [down]
    for step in range(LOG_LEAF - 1, -1, -1):
        below = []
        for t, parent in enumerate(targets):
            low = starts[step] + 2 * t
            mats = trans[low : low + 2].reshape(2 * rank, rank)
            both = coupled[low : low + 2].reshape(2 * rank, cols) + dot(mats, parent)
            both = both.astype(BF16)
            below += [both[:rank], both[rank:]]
        targets = below
    for t in range(0, leaves, 2):
        parts = [near_part[u] + dot(basis[u], targets[u]) for u in (t, t + 1)]
        turned = jnp.concatenate(parts, axis=0).T
        out[:, :, t * leaf_size : (t + 2) * leaf_size] = turned.reshape(
            operators, rhs_count, 2 * leaf_size
        )

    for d in range(1, leaf_count):
        leaf_copy(d, j).wait_send()
    for d in range(1, branch_count):
        branch_copy(d).wait_send()

    @pl.when(p < last)
    def _():
        for args in halos:
            halo(*args, 0).wait_send()

    @pl.when(p > 0)
    def _():
        for args in halos:
            halo(*args, 1).wait_send()


def solution(mesh):
    branch_count = mesh.shape["branch"]
    leaf_count = mesh.shape["leaf"]

    def per_device(
        values,
        leaf_basis,
        transfer,
        local_coupling,
        coupling_source,
        near_field,
        near_source,
        upper_transfer,
        upper_coupling,
        top_coupling,
    ):
        operators, rhs_count, width = values.shape
        cols = operators * rhs_count
        leaves, leaf_size, rank = leaf_basis.shape
        rows = transfer.shape[0]
        upper = upper_transfer.shape[1]
        any_spec = pl.BlockSpec(memory_space=pl.ANY)
        dma = pltpu.SemaphoreType.DMA

        def fixed(array):
            return pltpu.with_memory_space_constraint(array, pltpu.HBM)

        return pl.pallas_call(
            functools.partial(kernel, branch_count, leaf_count),
            out_shape=jax.ShapeDtypeStruct(values.shape, F32),
            in_specs=[any_spec] * 10,
            out_specs=pl.BlockSpec(memory_space=pltpu.VMEM),
            scratch_shapes=[
                pltpu.SMEM(coupling_source.shape, jnp.int32),
                pltpu.SMEM(near_source.shape, jnp.int32),
                pltpu.VMEM(values.shape, BF16),
                pltpu.VMEM(leaf_basis.shape, BF16),
                pltpu.VMEM(transfer.shape, BF16),
                pltpu.VMEM(local_coupling.shape, BF16),
                pltpu.VMEM(near_field.shape, BF16),
                pltpu.VMEM(upper_transfer.shape[1:], BF16),
                pltpu.VMEM((operators,) + upper_coupling.shape[2:], BF16),
                pltpu.VMEM((operators,) + top_coupling.shape[2:], BF16),
                pltpu.VMEM((3 * leaves, cols, 2 * leaf_size), BF16),
                pltpu.VMEM((3 * rows, cols, 2 * rank), BF16),
                pltpu.VMEM((leaf_count, rhs_count, operators * rank), BF16),
                pltpu.VMEM((upper - leaf_count, cols, rank), BF16),
                pltpu.VMEM((rhs_count, operators * rank), BF16),
                pltpu.VMEM((branch_count - 1, rhs_count, operators * rank), BF16),
                pltpu.VMEM((rows, rank, cols), F32),
                pltpu.VMEM((leaves, leaf_size, cols), F32),
                dma((10,)),
                dma((4,)),
                dma((4,)),
                dma((leaf_count - 1,)),
                dma((leaf_count - 1,)),
                dma((branch_count - 1,)),
                dma((branch_count - 1,)),
            ],
            compiler_params=pltpu.CompilerParams(
                collective_id=0, has_side_effects=True, vmem_limit_bytes=32 * 1024 * 1024
            ),
        )(
            fixed(values),
            fixed(leaf_basis),
            fixed(transfer),
            fixed(local_coupling),
            fixed(near_field),
            fixed(upper_transfer),
            fixed(upper_coupling),
            fixed(top_coupling),
            fixed(coupling_source),
            fixed(near_source),
        )

    in_specs = (
        P(None, None, ("branch", "leaf")),
        P(("branch", "leaf"), None, None),
        P(("branch", "leaf"), None, None),
        P(None, ("branch", "leaf"), None, None, None),
        P(("branch", "leaf"), None),
        P(None, ("branch", "leaf"), None, None, None),
        P(("branch", "leaf"), None),
        P("branch", None, None, None),
        P(None, "branch", None, None, None),
        P(None, "branch", None, None, None),
    )
    out_specs = P(None, None, ("branch", "leaf"))
    return jax.shard_map(
        per_device, mesh=mesh, in_specs=in_specs, out_specs=out_specs, check_vma=False
    )
```

```python
import functools

import jax
import jax.numpy as jnp
from jax import lax
from jax.experimental import pallas as pl
from jax.experimental.pallas import tpu as pltpu
from jax.sharding import PartitionSpec as P

LOG_LEAF = 3
F32 = jnp.float32
BF16 = jnp.bfloat16
MESH = pl.DeviceIdType.MESH


def dot(a, b):
    return jnp.dot(a, b, preferred_element_type=F32)


def dot_nt(a, b):
    return lax.dot_general(a, b, (((1,), (1,)), ((), ())), preferred_element_type=F32)


def side_by_side(blocks):
    pairs = []
    for i in range(0, len(blocks) - 1, 2):
        pairs.append(jnp.concatenate(blocks[i : i + 2], axis=1))
    if len(blocks) % 2:
        pairs.append(blocks[-1])
    return pairs[0] if len(pairs) == 1 else jnp.concatenate(pairs, axis=1)


def kernel(
    branch_count,
    leaf_count,
    values,
    leaf_basis,
    transfer,
    local_coupling,
    near_field,
    upper_transfer,
    upper_coupling,
    top_coupling,
    coupling_source,
    near_source,
    out,
    coupling_index,
    near_index,
    val,
    basis,
    trans,
    couple,
    near,
    up_trans,
    up_couple,
    top,
    value_win,
    coef_win,
    leaf_roots,
    upper,
    own_root,
    roots,
    coupled,
    near_part,
    load_sem,
    halo_send,
    halo_recv,
    leaf_send,
    leaf_recv,
    branch_send,
    branch_recv,
):
    operators, rhs_count, _ = val.shape
    cols = operators * rhs_count
    leaves, leaf_size, rank = basis.shape
    rows = trans.shape[0]
    cell_pairs, coef_pairs = leaves // 2, rows // 2
    blocks = couple.shape[2]
    near_blocks = near.shape[2]
    depth = leaf_count.bit_length() - 1
    b = lax.axis_index("branch")
    j = lax.axis_index("leaf")
    p = b * leaf_count + j
    last = branch_count * leaf_count - 1

    starts = [2 * leaves - 2 * (leaves >> level) for level in range(LOG_LEAF)]

    def dense(coef):
        return jnp.concatenate([coef[:rhs_count], coef[rhs_count:]], axis=1)

    def undense(coef):
        return jnp.concatenate([coef[:, :rank], coef[:, rank:]], axis=0)

    pieces = [
        (values, val),
        (leaf_basis, basis),
        (transfer, trans),
        (upper_transfer.at[0], up_trans),
        (near_source, near_index),
        (coupling_source, coupling_index),
        (near_field, near),
        (local_coupling, couple),
        (upper_coupling.at[:, 0], up_couple),
        (top_coupling.at[:, 0], top),
    ]
    loads = [
        pltpu.make_async_copy(src, dst, load_sem.at[i]) for i, (src, dst) in enumerate(pieces)
    ]
    for load in loads:
        load.start()
    val_load, basis_load, trans_load, ut_load, ni_load, ci_load = loads[:6]
    near_load, couple_load, uc_load, top_load = loads[6:]

    barrier = pltpu.get_barrier_semaphore()

    def greet(bb, jj):
        pl.semaphore_signal(barrier, inc=1, device_id=(bb, jj), device_id_type=MESH)

    for d in range(1, leaf_count):
        greet(b, lax.rem(j + d, leaf_count))
    for d in range(1, branch_count):
        greet(lax.rem(b + d, branch_count), j)
    low_edge = jnp.logical_and(j == 0, b > 0)
    high_edge = jnp.logical_and(j == leaf_count - 1, b < branch_count - 1)

    @pl.when(low_edge)
    def _():
        greet(b - 1, leaf_count - 1)

    @pl.when(high_edge)
    def _():
        greet(b + 1, 0)

    @pl.when(p == 0)
    def _():
        value_win[0:cell_pairs] = jnp.zeros((cell_pairs, cols, 2 * leaf_size), BF16)
        coef_win[0:coef_pairs] = jnp.zeros((coef_pairs, cols, 2 * rank), BF16)

    @pl.when(p == last)
    def _():
        value_win[2 * cell_pairs : 3 * cell_pairs] = jnp.zeros(
            (cell_pairs, cols, 2 * leaf_size), BF16
        )
        coef_win[2 * coef_pairs : 3 * coef_pairs] = jnp.zeros((coef_pairs, cols, 2 * rank), BF16)

    val_load.wait()
    cells = val[...].reshape(cols, leaves * leaf_size)
    for t in range(cell_pairs):
        value_win[cell_pairs + t] = cells[:, 2 * t * leaf_size : 2 * (t + 1) * leaf_size]

    greeted = leaf_count - 1 + branch_count - 1
    greeted += low_edge.astype(jnp.int32) + high_edge.astype(jnp.int32)
    pl.semaphore_wait(barrier, greeted)

    def halo(window, size, kind, way):
        place = 0 if way == 0 else 2 * size
        other = p + 1 if way == 0 else p - 1
        return pltpu.make_async_remote_copy(
            src_ref=window.at[pl.ds(size, size)],
            dst_ref=window.at[pl.ds(place, size)],
            send_sem=halo_send.at[2 * kind + way],
            recv_sem=halo_recv.at[2 * kind + way],
            device_id=(other // leaf_count, lax.rem(other, leaf_count)),
            device_id_type=MESH,
        )

    def for_ways(act):
        @pl.when(p < last)
        def _():
            act(0)

        @pl.when(p > 0)
        def _():
            act(1)

    def value_halo(way):
        return halo(value_win, cell_pairs, 0, way)

    def coef_halo(way):
        return halo(coef_win, coef_pairs, 1, way)

    for_ways(lambda way: value_halo(way).start())
    basis_load.wait()
    level = []
    for t in range(cell_pairs):
        pair = cells[:, 2 * t * leaf_size : 2 * (t + 1) * leaf_size]
        level.append(dot(pair[:, :leaf_size], basis[2 * t]).astype(BF16))
        level.append(dot(pair[:, leaf_size:], basis[2 * t + 1]).astype(BF16))
    trans_load.wait()
    for step in range(LOG_LEAF):
        above = []
        for t in range(leaves >> step + 1):
            low = starts[step] + 2 * t
            pair = side_by_side(level[2 * t : 2 * t + 2])
            coef_win[coef_pairs + low // 2] = pair
            mats = trans[low : low + 2].reshape(2 * rank, rank)
            above.append(dot(pair, mats).astype(BF16))
        level = above
    leaf_roots[j] = dense(level[0])

    def leaf_copy(d, slot):
        return pltpu.make_async_remote_copy(
            src_ref=leaf_roots.at[slot],
            dst_ref=leaf_roots.at[slot],
            send_sem=leaf_send.at[d - 1],
            recv_sem=leaf_recv.at[d - 1],
            device_id=(b, lax.rem(j + d, leaf_count)),
            device_id_type=MESH,
        )

    for d in range(1, leaf_count):
        leaf_copy(d, j).start()

    for_ways(lambda way: coef_halo(way).start())

    first = lax.broadcasted_iota(jnp.int32, (rank, cols), 1) < rhs_count

    def pick(both):
        return jnp.where(first, both[:rank], both[rank:])

    def turn(window, size):
        for m in range(3 * size):
            pair = window[m]
            half = pair.shape[1] // 2
            window[3 * size + m] = jnp.concatenate([pair[:, half:], pair[:, :half]], axis=1)

    def listed(matrices, row, count, window, source):
        wide = side_by_side(
            [matrices[:, row, m].reshape(operators * rank, rank) for m in range(count)]
        )
        picked = []
        for m in range(0, count, 2):
            half = window.shape[2] // 2
            left, right = window[source(m)], window[source(m + 1)]
            picked.append(jnp.concatenate([left[:, :half], right[:, half:]], axis=1))
        return pick(dot_nt(wide, jnp.concatenate(picked, axis=1)))

    for_ways(lambda way: value_halo(1 - way).wait_recv())
    turn(value_win, cell_pairs)
    ni_load.wait()
    near_load.wait()

    def near_step(t, carry):
        def source(m):
            s = near_index[t, m]
            return jnp.bitwise_and(s + m, 1) * 3 * cell_pairs + jnp.right_shift(s, 1)

        near_part[t] = listed(near, t, near_blocks, value_win, source)
        return carry

    lax.fori_loop(0, leaves, near_step, 0, unroll=4)

    ut_load.wait()
    for d in range(1, leaf_count):
        leaf_copy(d, lax.rem(j + leaf_count - d, leaf_count)).wait_recv()
    offsets = [2 * leaf_count - 2 * (leaf_count >> step) for step in range(depth + 1)]
    level = [undense(leaf_roots[m]) for m in range(leaf_count)]
    for step in range(depth):
        above = []
        for t in range(leaf_count >> step + 1):
            low = offsets[step] + 2 * t
            pair = side_by_side(level[2 * t : 2 * t + 2])
            mats = up_trans[low : low + 2].reshape(2 * rank, rank)
            coef = dot(pair, mats).astype(BF16)
            if step < depth - 1:
                upper[offsets[step + 1] - leaf_count + t] = coef
            above.append(coef)
        level = above
    own_root[...] = dense(level[0])

    def branch_copy(d):
        return pltpu.make_async_remote_copy(
            src_ref=own_root,
            dst_ref=roots.at[branch_count - 1 - d],
            send_sem=branch_send.at[d - 1],
            recv_sem=branch_recv.at[d - 1],
            device_id=(lax.rem(b + d, branch_count), j),
            device_id_type=MESH,
        )

    for d in range(1, branch_count):
        branch_copy(d).start()

    for_ways(lambda way: coef_halo(1 - way).wait_recv())
    turn(coef_win, coef_pairs)
    couple_load.wait()
    ci_load.wait()

    for step in range(LOG_LEAF):
        count = leaves >> step
        begin = starts[step]

        def couple_step(t, carry, count=count, begin=begin, shift=LOG_LEAF - step):
            row = begin + t

            def source(m):
                s = coupling_index[row, m]
                side = jnp.right_shift(s, shift)
                place = jnp.right_shift(jnp.bitwise_and(s, count - 1), 1)
                turned = jnp.bitwise_and(s + m, 1) * 3 * coef_pairs
                return turned + side * coef_pairs + begin // 2 + place

            coupled[row] = listed(couple, row, blocks, coef_win, source)
            return carry

        if step == 0:
            lax.fori_loop(0, count, couple_step, 0, unroll=4)
        else:
            for t in range(count):
                couple_step(t, 0)

    uc_load.wait()
    top_load.wait()
    sides = []
    for step in range(depth):
        own = jnp.right_shift(j, step)
        mats = up_couple[:, offsets[step] + own].reshape(operators * rank, rank)
        sibling = jnp.bitwise_xor(own, 1)
        if step == 0:
            sibling = undense(leaf_roots[sibling])
        else:
            sibling = upper[offsets[step] - leaf_count + sibling]
        sides.append(pick(dot_nt(mats, sibling)))

    for d in range(1, branch_count):
        branch_copy(d).wait_recv()
    tops = side_by_side(
        [top[:, m].reshape(operators * rank, rank) for m in range(branch_count - 1)]
    )
    others = side_by_side([undense(roots[m]) for m in range(branch_count - 1)])
    down = pick(dot_nt(tops, others)).astype(BF16)
    for step in range(depth - 1, -1, -1):
        mat = up_trans[offsets[step] + jnp.right_shift(j, step)]
        down = (sides[step] + dot(mat, down)).astype(BF16)
    targets = [down]
    for step in range(LOG_LEAF - 1, -1, -1):
        below = []
        for t, parent in enumerate(targets):
            low = starts[step] + 2 * t
            mats = trans[low : low + 2].reshape(2 * rank, rank)
            both = coupled[low : low + 2].reshape(2 * rank, cols) + dot(mats, parent)
            both = both.astype(BF16)
            below += [both[:rank], both[rank:]]
        targets = below
    for t in range(0, leaves, 2):
        parts = [near_part[u] + dot(basis[u], targets[u]) for u in (t, t + 1)]
        turned = jnp.concatenate(parts, axis=0).T
        out[:, :, t * leaf_size : (t + 2) * leaf_size] = turned.reshape(
            operators, rhs_count, 2 * leaf_size
        )

    for d in range(1, leaf_count):
        leaf_copy(d, j).wait_send()
    for d in range(1, branch_count):
        branch_copy(d).wait_send()

    for_ways(lambda way: value_halo(way).wait_send())
    for_ways(lambda way: coef_halo(way).wait_send())


def solution(mesh):
    branch_count = mesh.shape["branch"]
    leaf_count = mesh.shape["leaf"]

    def per_device(
        values,
        leaf_basis,
        transfer,
        local_coupling,
        coupling_source,
        near_field,
        near_source,
        upper_transfer,
        upper_coupling,
        top_coupling,
    ):
        operators, rhs_count, width = values.shape
        cols = operators * rhs_count
        leaves, leaf_size, rank = leaf_basis.shape
        rows = transfer.shape[0]
        upper = upper_transfer.shape[1]
        any_spec = pl.BlockSpec(memory_space=pl.ANY)
        dma = pltpu.SemaphoreType.DMA

        def fixed(array):
            return pltpu.with_memory_space_constraint(array, pltpu.HBM)

        return pl.pallas_call(
            functools.partial(kernel, branch_count, leaf_count),
            out_shape=jax.ShapeDtypeStruct(values.shape, F32),
            in_specs=[any_spec] * 10,
            out_specs=pl.BlockSpec(memory_space=pltpu.VMEM),
            scratch_shapes=[
                pltpu.SMEM(coupling_source.shape, jnp.int32),
                pltpu.SMEM(near_source.shape, jnp.int32),
                pltpu.VMEM(values.shape, BF16),
                pltpu.VMEM(leaf_basis.shape, BF16),
                pltpu.VMEM(transfer.shape, BF16),
                pltpu.VMEM(local_coupling.shape, BF16),
                pltpu.VMEM(near_field.shape, BF16),
                pltpu.VMEM(upper_transfer.shape[1:], BF16),
                pltpu.VMEM((operators,) + upper_coupling.shape[2:], BF16),
                pltpu.VMEM((operators,) + top_coupling.shape[2:], BF16),
                pltpu.VMEM((3 * leaves, cols, 2 * leaf_size), BF16),
                pltpu.VMEM((3 * rows, cols, 2 * rank), BF16),
                pltpu.VMEM((leaf_count, rhs_count, operators * rank), BF16),
                pltpu.VMEM((upper - leaf_count, cols, rank), BF16),
                pltpu.VMEM((rhs_count, operators * rank), BF16),
                pltpu.VMEM((branch_count - 1, rhs_count, operators * rank), BF16),
                pltpu.VMEM((rows, rank, cols), F32),
                pltpu.VMEM((leaves, leaf_size, cols), F32),
                dma((10,)),
                dma((4,)),
                dma((4,)),
                dma((leaf_count - 1,)),
                dma((leaf_count - 1,)),
                dma((branch_count - 1,)),
                dma((branch_count - 1,)),
            ],
            compiler_params=pltpu.CompilerParams(
                collective_id=0, has_side_effects=True, vmem_limit_bytes=32 * 1024 * 1024
            ),
        )(
            fixed(values),
            fixed(leaf_basis),
            fixed(transfer),
            fixed(local_coupling),
            fixed(near_field),
            fixed(upper_transfer),
            fixed(upper_coupling),
            fixed(top_coupling),
            fixed(coupling_source),
            fixed(near_source),
        )

    in_specs = (
        P(None, None, ("branch", "leaf")),
        P(("branch", "leaf"), None, None),
        P(("branch", "leaf"), None, None),
        P(None, ("branch", "leaf"), None, None, None),
        P(("branch", "leaf"), None),
        P(None, ("branch", "leaf"), None, None, None),
        P(("branch", "leaf"), None),
        P("branch", None, None, None),
        P(None, "branch", None, None, None),
        P(None, "branch", None, None, None),
    )
    out_specs = P(None, None, ("branch", "leaf"))
    return jax.shard_map(
        per_device, mesh=mesh, in_specs=in_specs, out_specs=out_specs, check_vma=False
    )
```

```python
import functools

import jax
import jax.numpy as jnp
from jax import lax
from jax.experimental import pallas as pl
from jax.experimental.pallas import tpu as pltpu
from jax.sharding import PartitionSpec as P

LOG_LEAF = 3
F32 = jnp.float32
BF16 = jnp.bfloat16
MESH = pl.DeviceIdType.MESH


def dot(a, b):
    return jnp.dot(a, b, preferred_element_type=F32)


def dot_nt(a, b):
    return lax.dot_general(a, b, (((1,), (1,)), ((), ())), preferred_element_type=F32)


def side_by_side(blocks):
    pairs = []
    for i in range(0, len(blocks) - 1, 2):
        pairs.append(jnp.concatenate(blocks[i : i + 2], axis=1))
    if len(blocks) % 2:
        pairs.append(blocks[-1])
    return pairs[0] if len(pairs) == 1 else jnp.concatenate(pairs, axis=1)


def kernel(
    branch_count,
    leaf_count,
    values,
    leaf_basis,
    transfer,
    local_coupling,
    near_field,
    upper_transfer,
    upper_coupling,
    top_coupling,
    coupling_source,
    near_source,
    out,
    coupling_index,
    near_index,
    val,
    basis,
    trans,
    couple,
    near,
    up_trans,
    up_couple,
    top,
    value_win,
    coef_win,
    leaf_roots,
    upper,
    own_root,
    roots,
    coupled,
    near_part,
    load_sem,
    halo_send,
    halo_recv,
    leaf_send,
    leaf_recv,
    branch_send,
    branch_recv,
):
    operators, rhs_count, _ = val.shape
    cols = operators * rhs_count
    leaves, leaf_size, rank = basis.shape
    rows = trans.shape[0]
    cell_pairs, coef_pairs = leaves // 2, rows // 2
    blocks = couple.shape[2]
    near_blocks = near.shape[2]
    depth = leaf_count.bit_length() - 1
    b = lax.axis_index("branch")
    j = lax.axis_index("leaf")
    p = b * leaf_count + j
    last = branch_count * leaf_count - 1

    starts = [2 * leaves - 2 * (leaves >> level) for level in range(LOG_LEAF)]

    def dense(coef):
        return jnp.concatenate([coef[:rhs_count], coef[rhs_count:]], axis=1)

    def undense(coef):
        return jnp.concatenate([coef[:, :rank], coef[:, rank:]], axis=0)

    half = leaves // 2
    chunks = [(0, half), (half, leaves)]
    pieces = [
        (values, val),
        (leaf_basis, basis),
        (transfer, trans),
        (upper_transfer.at[0], up_trans),
        (near_source, near_index),
        (coupling_source, coupling_index),
    ]
    for low, high in chunks:
        for g in range(operators):
            part = pl.ds(low, high - low)
            pieces.append((near_field.at[g, part], near.at[g, part]))
    pieces.append((upper_coupling.at[:, 0], up_couple))
    pieces.append((top_coupling.at[:, 0], top))
    chunks.append((leaves, rows))
    for low, high in chunks:
        for g in range(operators):
            part = pl.ds(low, high - low)
            pieces.append((local_coupling.at[g, part], couple.at[g, part]))
    loads = [
        pltpu.make_async_copy(src, dst, load_sem.at[i]) for i, (src, dst) in enumerate(pieces)
    ]
    for load in loads:
        load.start()
    val_load, basis_load, trans_load, ut_load, ni_load, ci_load = loads[:6]
    near_loads = loads[6 : 6 + 2 * operators]
    uc_load, top_load = loads[6 + 2 * operators : 8 + 2 * operators]
    couple_loads = loads[8 + 2 * operators :]

    barrier = pltpu.get_barrier_semaphore()

    def greet(bb, jj):
        pl.semaphore_signal(barrier, inc=1, device_id=(bb, jj), device_id_type=MESH)

    for d in range(1, leaf_count):
        greet(b, lax.rem(j + d, leaf_count))
    for d in range(1, branch_count):
        greet(lax.rem(b + d, branch_count), j)
    low_edge = jnp.logical_and(j == 0, b > 0)
    high_edge = jnp.logical_and(j == leaf_count - 1, b < branch_count - 1)

    @pl.when(low_edge)
    def _():
        greet(b - 1, leaf_count - 1)

    @pl.when(high_edge)
    def _():
        greet(b + 1, 0)

    @pl.when(p == 0)
    def _():
        value_win[0:cell_pairs] = jnp.zeros((cell_pairs, cols, 2 * leaf_size), BF16)
        coef_win[0:coef_pairs] = jnp.zeros((coef_pairs, cols, 2 * rank), BF16)

    @pl.when(p == last)
    def _():
        value_win[2 * cell_pairs : 3 * cell_pairs] = jnp.zeros(
            (cell_pairs, cols, 2 * leaf_size), BF16
        )
        coef_win[2 * coef_pairs : 3 * coef_pairs] = jnp.zeros((coef_pairs, cols, 2 * rank), BF16)

    val_load.wait()
    cells = val[...].reshape(cols, leaves * leaf_size)
    for t in range(cell_pairs):
        value_win[cell_pairs + t] = cells[:, 2 * t * leaf_size : 2 * (t + 1) * leaf_size]

    greeted = leaf_count - 1 + branch_count - 1
    greeted += low_edge.astype(jnp.int32) + high_edge.astype(jnp.int32)
    pl.semaphore_wait(barrier, greeted)

    def halo(window, size, kind, way):
        place = 0 if way == 0 else 2 * size
        other = p + 1 if way == 0 else p - 1
        return pltpu.make_async_remote_copy(
            src_ref=window.at[pl.ds(size, size)],
            dst_ref=window.at[pl.ds(place, size)],
            send_sem=halo_send.at[2 * kind + way],
            recv_sem=halo_recv.at[2 * kind + way],
            device_id=(other // leaf_count, lax.rem(other, leaf_count)),
            device_id_type=MESH,
        )

    def for_ways(act):
        @pl.when(p < last)
        def _():
            act(0)

        @pl.when(p > 0)
        def _():
            act(1)

    def value_halo(way):
        return halo(value_win, cell_pairs, 0, way)

    def coef_halo(way):
        return halo(coef_win, coef_pairs, 1, way)

    for_ways(lambda way: value_halo(way).start())
    basis_load.wait()
    level = []
    for t in range(cell_pairs):
        pair = cells[:, 2 * t * leaf_size : 2 * (t + 1) * leaf_size]
        level.append(dot(pair[:, :leaf_size], basis[2 * t]).astype(BF16))
        level.append(dot(pair[:, leaf_size:], basis[2 * t + 1]).astype(BF16))
    trans_load.wait()
    for step in range(LOG_LEAF):
        above = []
        for t in range(leaves >> step + 1):
            low = starts[step] + 2 * t
            pair = side_by_side(level[2 * t : 2 * t + 2])
            coef_win[coef_pairs + low // 2] = pair
            mats = trans[low : low + 2].reshape(2 * rank, rank)
            above.append(dot(pair, mats).astype(BF16))
        level = above
    leaf_roots[j] = dense(level[0])

    def leaf_copy(d, slot):
        return pltpu.make_async_remote_copy(
            src_ref=leaf_roots.at[slot],
            dst_ref=leaf_roots.at[slot],
            send_sem=leaf_send.at[d - 1],
            recv_sem=leaf_recv.at[d - 1],
            device_id=(b, lax.rem(j + d, leaf_count)),
            device_id_type=MESH,
        )

    for d in range(1, leaf_count):
        leaf_copy(d, j).start()

    for_ways(lambda way: coef_halo(way).start())

    first = lax.broadcasted_iota(jnp.int32, (rank, cols), 1) < rhs_count

    def pick(both):
        return jnp.where(first, both[:rank], both[rank:])

    def turn(window, size):
        for m in range(3 * size):
            pair = window[m]
            half = pair.shape[1] // 2
            window[3 * size + m] = jnp.concatenate([pair[:, half:], pair[:, :half]], axis=1)

    def listed(matrices, row, count, window, source):
        wide = side_by_side(
            [matrices[:, row, m].reshape(operators * rank, rank) for m in range(count)]
        )
        picked = []
        for m in range(0, count, 2):
            half = window.shape[2] // 2
            left, right = window[source(m)], window[source(m + 1)]
            picked.append(jnp.concatenate([left[:, :half], right[:, half:]], axis=1))
        return pick(dot_nt(wide, jnp.concatenate(picked, axis=1)))

    for_ways(lambda way: value_halo(1 - way).wait_recv())
    turn(value_win, cell_pairs)
    ni_load.wait()

    def near_step(t, carry):
        def source(m):
            s = near_index[t, m]
            return jnp.bitwise_and(s + m, 1) * 3 * cell_pairs + jnp.right_shift(s, 1)

        near_part[t] = listed(near, t, near_blocks, value_win, source)
        return carry

    for i, (low, high) in enumerate(chunks[:2]):
        for load in near_loads[i * operators : (i + 1) * operators]:
            load.wait()
        for t in range(low, high):
            near_step(t, 0)

    ut_load.wait()
    for d in range(1, leaf_count):
        leaf_copy(d, lax.rem(j + leaf_count - d, leaf_count)).wait_recv()
    offsets = [2 * leaf_count - 2 * (leaf_count >> step) for step in range(depth + 1)]
    level = [undense(leaf_roots[m]) for m in range(leaf_count)]
    for step in range(depth):
        above = []
        for t in range(leaf_count >> step + 1):
            low = offsets[step] + 2 * t
            pair = side_by_side(level[2 * t : 2 * t + 2])
            mats = up_trans[low : low + 2].reshape(2 * rank, rank)
            coef = dot(pair, mats).astype(BF16)
            if step < depth - 1:
                upper[offsets[step + 1] - leaf_count + t] = coef
            above.append(coef)
        level = above
    own_root[...] = dense(level[0])

    def branch_copy(d):
        return pltpu.make_async_remote_copy(
            src_ref=own_root,
            dst_ref=roots.at[branch_count - 1 - d],
            send_sem=branch_send.at[d - 1],
            recv_sem=branch_recv.at[d - 1],
            device_id=(lax.rem(b + d, branch_count), j),
            device_id_type=MESH,
        )

    for d in range(1, branch_count):
        branch_copy(d).start()

    uc_load.wait()
    top_load.wait()
    sides = []
    for step in range(depth):
        own = jnp.right_shift(j, step)
        mats = up_couple[:, offsets[step] + own].reshape(operators * rank, rank)
        sibling = jnp.bitwise_xor(own, 1)
        if step == 0:
            sibling = undense(leaf_roots[sibling])
        else:
            sibling = upper[offsets[step] - leaf_count + sibling]
        sides.append(pick(dot_nt(mats, sibling)))

    for_ways(lambda way: coef_halo(1 - way).wait_recv())
    turn(coef_win, coef_pairs)
    ci_load.wait()

    for step in range(LOG_LEAF):
        count = leaves >> step
        begin = starts[step]

        def couple_step(t, carry, count=count, begin=begin, shift=LOG_LEAF - step):
            row = begin + t

            def source(m):
                s = coupling_index[row, m]
                side = jnp.right_shift(s, shift)
                place = jnp.right_shift(jnp.bitwise_and(s, count - 1), 1)
                turned = jnp.bitwise_and(s + m, 1) * 3 * coef_pairs
                return turned + side * coef_pairs + begin // 2 + place

            coupled[row] = listed(couple, row, blocks, coef_win, source)
            return carry

        for t in range(count):
            for i, (low, _) in enumerate(chunks):
                if begin + t == low:
                    for load in couple_loads[i * operators : (i + 1) * operators]:
                        load.wait()
            couple_step(t, 0)

    for d in range(1, branch_count):
        branch_copy(d).wait_recv()
    tops = side_by_side(
        [top[:, m].reshape(operators * rank, rank) for m in range(branch_count - 1)]
    )
    others = side_by_side([undense(roots[m]) for m in range(branch_count - 1)])
    down = pick(dot_nt(tops, others)).astype(BF16)
    for step in range(depth - 1, -1, -1):
        mat = up_trans[offsets[step] + jnp.right_shift(j, step)]
        down = (sides[step] + dot(mat, down)).astype(BF16)
    targets = [down]
    for step in range(LOG_LEAF - 1, -1, -1):
        below = []
        for t, parent in enumerate(targets):
            low = starts[step] + 2 * t
            mats = trans[low : low + 2].reshape(2 * rank, rank)
            both = coupled[low : low + 2].reshape(2 * rank, cols) + dot(mats, parent)
            both = both.astype(BF16)
            below += [both[:rank], both[rank:]]
        targets = below
    for t in range(0, leaves, 2):
        parts = [near_part[u] + dot(basis[u], targets[u]) for u in (t, t + 1)]
        turned = jnp.concatenate(parts, axis=0).T
        out[:, :, t * leaf_size : (t + 2) * leaf_size] = turned.reshape(
            operators, rhs_count, 2 * leaf_size
        )

    for d in range(1, leaf_count):
        leaf_copy(d, j).wait_send()
    for d in range(1, branch_count):
        branch_copy(d).wait_send()

    for_ways(lambda way: value_halo(way).wait_send())
    for_ways(lambda way: coef_halo(way).wait_send())


def solution(mesh):
    branch_count = mesh.shape["branch"]
    leaf_count = mesh.shape["leaf"]

    def per_device(
        values,
        leaf_basis,
        transfer,
        local_coupling,
        coupling_source,
        near_field,
        near_source,
        upper_transfer,
        upper_coupling,
        top_coupling,
    ):
        operators, rhs_count, width = values.shape
        cols = operators * rhs_count
        leaves, leaf_size, rank = leaf_basis.shape
        rows = transfer.shape[0]
        upper = upper_transfer.shape[1]
        any_spec = pl.BlockSpec(memory_space=pl.ANY)
        dma = pltpu.SemaphoreType.DMA

        def fixed(array):
            return pltpu.with_memory_space_constraint(array, pltpu.HBM)

        return pl.pallas_call(
            functools.partial(kernel, branch_count, leaf_count),
            out_shape=jax.ShapeDtypeStruct(values.shape, F32),
            in_specs=[any_spec] * 10,
            out_specs=pl.BlockSpec(memory_space=pltpu.VMEM),
            scratch_shapes=[
                pltpu.SMEM(coupling_source.shape, jnp.int32),
                pltpu.SMEM(near_source.shape, jnp.int32),
                pltpu.VMEM(values.shape, BF16),
                pltpu.VMEM(leaf_basis.shape, BF16),
                pltpu.VMEM(transfer.shape, BF16),
                pltpu.VMEM(local_coupling.shape, BF16),
                pltpu.VMEM(near_field.shape, BF16),
                pltpu.VMEM(upper_transfer.shape[1:], BF16),
                pltpu.VMEM((operators,) + upper_coupling.shape[2:], BF16),
                pltpu.VMEM((operators,) + top_coupling.shape[2:], BF16),
                pltpu.VMEM((3 * leaves, cols, 2 * leaf_size), BF16),
                pltpu.VMEM((3 * rows, cols, 2 * rank), BF16),
                pltpu.VMEM((leaf_count, rhs_count, operators * rank), BF16),
                pltpu.VMEM((upper - leaf_count, cols, rank), BF16),
                pltpu.VMEM((rhs_count, operators * rank), BF16),
                pltpu.VMEM((branch_count - 1, rhs_count, operators * rank), BF16),
                pltpu.VMEM((rows, rank, cols), F32),
                pltpu.VMEM((leaves, leaf_size, cols), F32),
                dma((8 + 5 * operators,)),
                dma((4,)),
                dma((4,)),
                dma((leaf_count - 1,)),
                dma((leaf_count - 1,)),
                dma((branch_count - 1,)),
                dma((branch_count - 1,)),
            ],
            compiler_params=pltpu.CompilerParams(
                collective_id=0, has_side_effects=True, vmem_limit_bytes=32 * 1024 * 1024
            ),
        )(
            fixed(values),
            fixed(leaf_basis),
            fixed(transfer),
            fixed(local_coupling),
            fixed(near_field),
            fixed(upper_transfer),
            fixed(upper_coupling),
            fixed(top_coupling),
            fixed(coupling_source),
            fixed(near_source),
        )

    in_specs = (
        P(None, None, ("branch", "leaf")),
        P(("branch", "leaf"), None, None),
        P(("branch", "leaf"), None, None),
        P(None, ("branch", "leaf"), None, None, None),
        P(("branch", "leaf"), None),
        P(None, ("branch", "leaf"), None, None, None),
        P(("branch", "leaf"), None),
        P("branch", None, None, None),
        P(None, "branch", None, None, None),
        P(None, "branch", None, None, None),
    )
    out_specs = P(None, None, ("branch", "leaf"))
    return jax.shard_map(
        per_device, mesh=mesh, in_specs=in_specs, out_specs=out_specs, check_vma=False
    )
```

```python
import functools

import jax
import jax.numpy as jnp
from jax import lax
from jax.experimental import pallas as pl
from jax.experimental.pallas import tpu as pltpu
from jax.sharding import PartitionSpec as P

LOG_LEAF = 3
F32 = jnp.float32
BF16 = jnp.bfloat16
MESH = pl.DeviceIdType.MESH


def dot(a, b):
    return jnp.dot(a, b, preferred_element_type=F32)


def dot_nt(a, b):
    return lax.dot_general(a, b, (((1,), (1,)), ((), ())), preferred_element_type=F32)


def side_by_side(blocks):
    pairs = []
    for i in range(0, len(blocks) - 1, 2):
        pairs.append(jnp.concatenate(blocks[i : i + 2], axis=1))
    if len(blocks) % 2:
        pairs.append(blocks[-1])
    return pairs[0] if len(pairs) == 1 else jnp.concatenate(pairs, axis=1)


def kernel(
    branch_count,
    leaf_count,
    values,
    leaf_basis,
    transfer,
    local_coupling,
    near_field,
    upper_transfer,
    upper_coupling,
    top_coupling,
    coupling_source,
    near_source,
    out,
    coupling_index,
    near_index,
    val,
    basis,
    trans,
    couple,
    near,
    up_trans,
    up_couple,
    top,
    value_win,
    coef_win,
    leaf_roots,
    paths,
    upper,
    own_root,
    roots,
    near_part,
    load_sem,
    halo_send,
    halo_recv,
    leaf_send,
    leaf_recv,
    branch_send,
    branch_recv,
):
    operators, rhs_count, _ = val.shape
    cols = operators * rhs_count
    leaves, leaf_size, rank = basis.shape
    rows = trans.shape[0]
    cell_pairs, coef_pairs = leaves // 2, rows // 2
    blocks = couple.shape[2]
    near_blocks = near.shape[2]
    depth = leaf_count.bit_length() - 1
    b = lax.axis_index("branch")
    j = lax.axis_index("leaf")
    p = b * leaf_count + j
    last = branch_count * leaf_count - 1

    starts = [2 * leaves - 2 * (leaves >> level) for level in range(LOG_LEAF)]

    def dense(coef):
        return jnp.concatenate([coef[:rhs_count], coef[rhs_count:]], axis=1)

    def undense(coef):
        return jnp.concatenate([coef[:, :rank], coef[:, rank:]], axis=0)

    half = leaves // 2
    chunks = [(0, half), (half, leaves)]
    pieces = [
        (values, val),
        (leaf_basis, basis),
        (transfer, trans),
        (upper_transfer.at[0], up_trans),
        (near_source, near_index),
        (coupling_source, coupling_index),
    ]
    for low, high in chunks:
        for g in range(operators):
            part = pl.ds(low, high - low)
            pieces.append((near_field.at[g, part], near.at[g, part]))
    pieces.append((upper_coupling.at[:, 0], up_couple))
    pieces.append((top_coupling.at[:, 0], top))
    for low, high in ((leaves, rows), (0, leaves)):
        for g in range(operators):
            part = pl.ds(low, high - low)
            pieces.append((local_coupling.at[g, part], couple.at[g, part]))
    loads = [
        pltpu.make_async_copy(src, dst, load_sem.at[i]) for i, (src, dst) in enumerate(pieces)
    ]
    for load in loads[:3]:
        load.start()
    val_load, basis_load, trans_load, ut_load, ni_load, ci_load = loads[:6]
    near_loads = loads[6 : 6 + 2 * operators]
    uc_load, top_load = loads[6 + 2 * operators : 8 + 2 * operators]
    couple_loads = loads[8 + 2 * operators :]

    barrier = pltpu.get_barrier_semaphore()

    def greet(bb, jj):
        pl.semaphore_signal(barrier, inc=1, device_id=(bb, jj), device_id_type=MESH)

    for d in range(1, leaf_count):
        greet(b, lax.rem(j + d, leaf_count))
    for d in range(1, branch_count):
        greet(lax.rem(b + d, branch_count), j)
    low_edge = jnp.logical_and(j == 0, b > 0)
    high_edge = jnp.logical_and(j == leaf_count - 1, b < branch_count - 1)

    @pl.when(low_edge)
    def _():
        greet(b - 1, leaf_count - 1)

    @pl.when(high_edge)
    def _():
        greet(b + 1, 0)

    for load in loads[3:]:
        load.start()

    @pl.when(p == 0)
    def _():
        value_win[0:cell_pairs] = jnp.zeros((cell_pairs, cols, 2 * leaf_size), BF16)
        coef_win[0:coef_pairs] = jnp.zeros((coef_pairs, cols, 2 * rank), BF16)

    @pl.when(p == last)
    def _():
        value_win[2 * cell_pairs : 3 * cell_pairs] = jnp.zeros(
            (cell_pairs, cols, 2 * leaf_size), BF16
        )
        coef_win[2 * coef_pairs : 3 * coef_pairs] = jnp.zeros((coef_pairs, cols, 2 * rank), BF16)

    val_load.wait()
    cells = val[...].reshape(cols, leaves * leaf_size)
    for t in range(cell_pairs):
        value_win[cell_pairs + t] = cells[:, 2 * t * leaf_size : 2 * (t + 1) * leaf_size]

    greeted = leaf_count - 1 + branch_count - 1
    greeted += low_edge.astype(jnp.int32) + high_edge.astype(jnp.int32)
    pl.semaphore_wait(barrier, greeted)

    def halo(window, size, kind, way):
        place = 0 if way == 0 else 2 * size
        other = p + 1 if way == 0 else p - 1
        return pltpu.make_async_remote_copy(
            src_ref=window.at[pl.ds(size, size)],
            dst_ref=window.at[pl.ds(place, size)],
            send_sem=halo_send.at[2 * kind + way],
            recv_sem=halo_recv.at[2 * kind + way],
            device_id=(other // leaf_count, lax.rem(other, leaf_count)),
            device_id_type=MESH,
        )

    def for_ways(act):
        @pl.when(p < last)
        def _():
            act(0)

        @pl.when(p > 0)
        def _():
            act(1)

    def value_halo(way):
        return halo(value_win, cell_pairs, 0, way)

    def coef_halo(way):
        return halo(coef_win, coef_pairs, 1, way)

    for_ways(lambda way: value_halo(way).start())
    basis_load.wait()
    level = []
    for t in range(cell_pairs):
        pair = cells[:, 2 * t * leaf_size : 2 * (t + 1) * leaf_size]
        level.append(dot(pair[:, :leaf_size], basis[2 * t]).astype(BF16))
        level.append(dot(pair[:, leaf_size:], basis[2 * t + 1]).astype(BF16))
    trans_load.wait()
    for step in range(LOG_LEAF):
        above = []
        for t in range(leaves >> step + 1):
            low = starts[step] + 2 * t
            pair = side_by_side(level[2 * t : 2 * t + 2])
            coef_win[coef_pairs + low // 2] = pair
            mats = trans[low : low + 2].reshape(2 * rank, rank)
            above.append(dot(pair, mats).astype(BF16))
        level = above
    leaf_roots[j] = dense(level[0])

    def leaf_copy(d, slot):
        return pltpu.make_async_remote_copy(
            src_ref=leaf_roots.at[slot],
            dst_ref=leaf_roots.at[slot],
            send_sem=leaf_send.at[d - 1],
            recv_sem=leaf_recv.at[d - 1],
            device_id=(b, lax.rem(j + d, leaf_count)),
            device_id_type=MESH,
        )

    for d in range(1, leaf_count):
        leaf_copy(d, j).start()

    for_ways(lambda way: coef_halo(way).start())

    first = lax.broadcasted_iota(jnp.int32, (rank, cols), 1) < rhs_count

    def pick(both):
        return jnp.where(first, both[:rank], both[rank:])

    def turn(window, size):
        for m in range(3 * size):
            pair = window[m]
            half = pair.shape[1] // 2
            window[3 * size + m] = jnp.concatenate([pair[:, half:], pair[:, :half]], axis=1)

    def listed(matrices, row, count, window, source):
        wide = side_by_side(
            [matrices[:, row, m].reshape(operators * rank, rank) for m in range(count)]
        )
        picked = []
        for m in range(0, count, 2):
            half = window.shape[2] // 2
            left, right = window[source(m)], window[source(m + 1)]
            picked.append(jnp.concatenate([left[:, :half], right[:, half:]], axis=1))
        return pick(dot_nt(wide, jnp.concatenate(picked, axis=1)))

    ut_load.wait()
    offsets = [2 * leaf_count - 2 * (leaf_count >> step) for step in range(depth + 1)]
    above = [up_trans[offsets[depth] - 2], up_trans[offsets[depth] - 1]]
    for step in range(depth - 2, -1, -1):
        below = []
        for t, path in enumerate(above):
            low = offsets[step] + 2 * t
            mats = up_trans[low : low + 2].reshape(2 * rank, rank)
            both = dot(mats, path).astype(BF16)
            below += [both[:rank], both[rank:]]
        above = below
    for t, path in enumerate(above):
        paths[t] = path

    for_ways(lambda way: value_halo(1 - way).wait_recv())
    turn(value_win, cell_pairs)
    ni_load.wait()

    def near_step(t, carry):
        def source(m):
            s = near_index[t, m]
            return jnp.bitwise_and(s + m, 1) * 3 * cell_pairs + jnp.right_shift(s, 1)

        near_part[t] = listed(near, t, near_blocks, value_win, source)
        return carry

    for i, (low, high) in enumerate(chunks):
        for load in near_loads[i * operators : (i + 1) * operators]:
            load.wait()
        for t in range(low, high):
            near_step(t, 0)

    for d in range(1, leaf_count):
        leaf_copy(d, lax.rem(j + leaf_count - d, leaf_count)).wait_recv()
    level = [undense(leaf_roots[m]) for m in range(leaf_count)]
    root = dot(side_by_side(level), paths[...].reshape(leaf_count * rank, rank))
    own_root[...] = dense(root.astype(BF16))

    def branch_copy(d):
        return pltpu.make_async_remote_copy(
            src_ref=own_root,
            dst_ref=roots.at[branch_count - 1 - d],
            send_sem=branch_send.at[d - 1],
            recv_sem=branch_recv.at[d - 1],
            device_id=(lax.rem(b + d, branch_count), j),
            device_id_type=MESH,
        )

    for d in range(1, branch_count):
        branch_copy(d).start()

    for step in range(depth - 1):
        above = []
        for t in range(leaf_count >> step + 1):
            low = offsets[step] + 2 * t
            pair = side_by_side(level[2 * t : 2 * t + 2])
            mats = up_trans[low : low + 2].reshape(2 * rank, rank)
            coef = dot(pair, mats).astype(BF16)
            upper[offsets[step + 1] - leaf_count + t] = coef
            above.append(coef)
        level = above

    uc_load.wait()
    top_load.wait()
    sides = []
    for step in range(depth):
        own = jnp.right_shift(j, step)
        mats = up_couple[:, offsets[step] + own].reshape(operators * rank, rank)
        sibling = jnp.bitwise_xor(own, 1)
        if step == 0:
            sibling = undense(leaf_roots[sibling])
        else:
            sibling = upper[offsets[step] - leaf_count + sibling]
        sides.append(pick(dot_nt(mats, sibling)))

    for_ways(lambda way: coef_halo(1 - way).wait_recv())
    turn(coef_win, coef_pairs)
    ci_load.wait()

    rest = sides[depth - 1].astype(BF16)
    for step in range(depth - 2, -1, -1):
        mat = up_trans[offsets[step] + jnp.right_shift(j, step)]
        rest = (sides[step] + dot(mat, rest)).astype(BF16)
    targets = [jnp.concatenate([rest, paths[j]], axis=1)]
    blank = jnp.zeros((2 * rank, rank), F32)

    def couple_row(row, shift):
        count = 1 << shift

        def source(m):
            s = coupling_index[row, m]
            side = jnp.right_shift(s, shift)
            place = jnp.right_shift(jnp.bitwise_and(s, count - 1), 1)
            turned = jnp.bitwise_and(s + m, 1) * 3 * coef_pairs
            return turned + side * coef_pairs + leaves - count + place

        return listed(couple, row, blocks, coef_win, source)

    known, from_top = [], []
    for step in range(LOG_LEAF - 1, -1, -1):
        if step == LOG_LEAF - 1:
            for load in couple_loads[:operators]:
                load.wait()
        if step == 0:
            for load in couple_loads[operators:]:
                load.wait()
        below = []
        for t, parent in enumerate(targets):
            low = starts[step] + 2 * t
            mats = trans[low : low + 2].reshape(2 * rank, rank)
            pair = [couple_row(low + u, LOG_LEAF - step) for u in range(2)]
            both = jnp.concatenate([jnp.concatenate(pair, axis=0), blank], axis=1)
            both = (both + dot(mats, parent)).astype(BF16)
            children = [both[:rank], both[rank:]]
            below += children
            if step == 0:
                parts = []
                for u in range(2):
                    far = dot(basis[low + u], children[u])
                    parts.append(near_part[low + u] + far[:, :cols])
                    from_top.append(far[:, cols:].astype(BF16))
                known.append(jnp.concatenate(parts, axis=0).T)
        targets = below
    tops = side_by_side(
        [top[:, m].reshape(operators * rank, rank) for m in range(branch_count - 1)]
    )

    for d in range(1, branch_count):
        branch_copy(d).wait_recv()
    others = side_by_side([undense(roots[m]) for m in range(branch_count - 1)])
    crossed = dot_nt(others, tops)
    down = jnp.concatenate([crossed[:rhs_count, :rank], crossed[rhs_count:, rank:]], axis=0)
    down = down.astype(BF16)
    for t in range(0, leaves, 2):
        mats = jnp.concatenate(from_top[t : t + 2], axis=0)
        both = known[t // 2] + dot_nt(down, mats)
        out[:, :, t * leaf_size : (t + 2) * leaf_size] = both.reshape(
            operators, rhs_count, 2 * leaf_size
        )

    for d in range(1, leaf_count):
        leaf_copy(d, j).wait_send()
    for d in range(1, branch_count):
        branch_copy(d).wait_send()

    for_ways(lambda way: value_halo(way).wait_send())
    for_ways(lambda way: coef_halo(way).wait_send())


def solution(mesh):
    branch_count = mesh.shape["branch"]
    leaf_count = mesh.shape["leaf"]

    def per_device(
        values,
        leaf_basis,
        transfer,
        local_coupling,
        coupling_source,
        near_field,
        near_source,
        upper_transfer,
        upper_coupling,
        top_coupling,
    ):
        operators, rhs_count, width = values.shape
        cols = operators * rhs_count
        leaves, leaf_size, rank = leaf_basis.shape
        rows = transfer.shape[0]
        upper = upper_transfer.shape[1]
        any_spec = pl.BlockSpec(memory_space=pl.ANY)
        dma = pltpu.SemaphoreType.DMA

        def fixed(array):
            return pltpu.with_memory_space_constraint(array, pltpu.HBM)

        return pl.pallas_call(
            functools.partial(kernel, branch_count, leaf_count),
            out_shape=jax.ShapeDtypeStruct(values.shape, F32),
            in_specs=[any_spec] * 10,
            out_specs=pl.BlockSpec(memory_space=pltpu.VMEM),
            scratch_shapes=[
                pltpu.SMEM(coupling_source.shape, jnp.int32),
                pltpu.SMEM(near_source.shape, jnp.int32),
                pltpu.VMEM(values.shape, BF16),
                pltpu.VMEM(leaf_basis.shape, BF16),
                pltpu.VMEM(transfer.shape, BF16),
                pltpu.VMEM(local_coupling.shape, BF16),
                pltpu.VMEM(near_field.shape, BF16),
                pltpu.VMEM(upper_transfer.shape[1:], BF16),
                pltpu.VMEM((operators,) + upper_coupling.shape[2:], BF16),
                pltpu.VMEM((operators,) + top_coupling.shape[2:], BF16),
                pltpu.VMEM((3 * leaves, cols, 2 * leaf_size), BF16),
                pltpu.VMEM((3 * rows, cols, 2 * rank), BF16),
                pltpu.VMEM((leaf_count, rhs_count, operators * rank), BF16),
                pltpu.VMEM((leaf_count, rank, rank), BF16),
                pltpu.VMEM((upper - leaf_count, cols, rank), BF16),
                pltpu.VMEM((rhs_count, operators * rank), BF16),
                pltpu.VMEM((branch_count - 1, rhs_count, operators * rank), BF16),
                pltpu.VMEM((leaves, leaf_size, cols), F32),
                dma((8 + 4 * operators,)),
                dma((4,)),
                dma((4,)),
                dma((leaf_count - 1,)),
                dma((leaf_count - 1,)),
                dma((branch_count - 1,)),
                dma((branch_count - 1,)),
            ],
            compiler_params=pltpu.CompilerParams(
                collective_id=0, has_side_effects=True, vmem_limit_bytes=32 * 1024 * 1024
            ),
        )(
            fixed(values),
            fixed(leaf_basis),
            fixed(transfer),
            fixed(local_coupling),
            fixed(near_field),
            fixed(upper_transfer),
            fixed(upper_coupling),
            fixed(top_coupling),
            fixed(coupling_source),
            fixed(near_source),
        )

    in_specs = (
        P(None, None, ("branch", "leaf")),
        P(("branch", "leaf"), None, None),
        P(("branch", "leaf"), None, None),
        P(None, ("branch", "leaf"), None, None, None),
        P(("branch", "leaf"), None),
        P(None, ("branch", "leaf"), None, None, None),
        P(("branch", "leaf"), None),
        P("branch", None, None, None),
        P(None, "branch", None, None, None),
        P(None, "branch", None, None, None),
    )
    out_specs = P(None, None, ("branch", "leaf"))
    return jax.shard_map(
        per_device, mesh=mesh, in_specs=in_specs, out_specs=out_specs, check_vma=False
    )
```

```python
import functools

import jax
import jax.numpy as jnp
from jax import lax
from jax.experimental import pallas as pl
from jax.experimental.pallas import tpu as pltpu
from jax.sharding import PartitionSpec as P

LOG_LEAF = 3
F32 = jnp.float32
BF16 = jnp.bfloat16
MESH = pl.DeviceIdType.MESH


def dot(a, b):
    return jnp.dot(a, b, preferred_element_type=F32)


def dot_nt(a, b):
    return lax.dot_general(a, b, (((1,), (1,)), ((), ())), preferred_element_type=F32)


def side_by_side(blocks):
    pairs = []
    for i in range(0, len(blocks) - 1, 2):
        pairs.append(jnp.concatenate(blocks[i : i + 2], axis=1))
    if len(blocks) % 2:
        pairs.append(blocks[-1])
    return pairs[0] if len(pairs) == 1 else jnp.concatenate(pairs, axis=1)


def kernel(
    branch_count,
    leaf_count,
    values,
    leaf_basis,
    transfer,
    local_coupling,
    near_field,
    upper_transfer,
    upper_coupling,
    top_coupling,
    coupling_source,
    near_source,
    out,
    coupling_index,
    near_index,
    val,
    basis,
    trans,
    couple,
    near,
    up_trans,
    up_couple,
    top,
    value_win,
    coef_win,
    value_table,
    coef_table,
    leaf_roots,
    paths,
    upper,
    own_root,
    roots,
    near_part,
    load_sem,
    halo_send,
    halo_recv,
    leaf_send,
    leaf_recv,
    branch_send,
    branch_recv,
):
    operators, rhs_count, _ = val.shape
    cols = operators * rhs_count
    leaves, leaf_size, rank = basis.shape
    rows = trans.shape[0]
    cell_pairs, coef_pairs = leaves // 2, rows // 2
    blocks = couple.shape[2]
    near_blocks = near.shape[2]
    depth = leaf_count.bit_length() - 1
    b = lax.axis_index("branch")
    j = lax.axis_index("leaf")
    p = b * leaf_count + j
    last = branch_count * leaf_count - 1

    starts = [2 * leaves - 2 * (leaves >> level) for level in range(LOG_LEAF)]

    def dense(coef):
        return jnp.concatenate([coef[:rhs_count], coef[rhs_count:]], axis=1)

    def undense(coef):
        return jnp.concatenate([coef[:, :rank], coef[:, rank:]], axis=0)

    half = leaves // 2
    chunks = [(0, half), (half, leaves)]
    pieces = [
        (values, val),
        (leaf_basis, basis),
        (transfer, trans),
        (upper_transfer.at[0], up_trans),
        (near_source, near_index),
        (coupling_source, coupling_index),
    ]
    for low, high in chunks:
        for g in range(operators):
            part = pl.ds(low, high - low)
            pieces.append((near_field.at[g, part], near.at[g, part]))
    pieces.append((upper_coupling.at[:, 0], up_couple))
    pieces.append((top_coupling.at[:, 0], top))
    for low, high in ((leaves, rows), (0, leaves)):
        for g in range(operators):
            part = pl.ds(low, high - low)
            pieces.append((local_coupling.at[g, part], couple.at[g, part]))
    loads = [
        pltpu.make_async_copy(src, dst, load_sem.at[i]) for i, (src, dst) in enumerate(pieces)
    ]
    for load in loads[:3]:
        load.start()
    val_load, basis_load, trans_load, ut_load, ni_load, ci_load = loads[:6]
    near_loads = loads[6 : 6 + 2 * operators]
    uc_load, top_load = loads[6 + 2 * operators : 8 + 2 * operators]
    couple_loads = loads[8 + 2 * operators :]

    barrier = pltpu.get_barrier_semaphore()

    def greet(bb, jj):
        pl.semaphore_signal(barrier, inc=1, device_id=(bb, jj), device_id_type=MESH)

    for d in range(1, leaf_count):
        greet(b, lax.rem(j + d, leaf_count))
    for d in range(1, branch_count):
        greet(lax.rem(b + d, branch_count), j)
    low_edge = jnp.logical_and(j == 0, b > 0)
    high_edge = jnp.logical_and(j == leaf_count - 1, b < branch_count - 1)

    @pl.when(low_edge)
    def _():
        greet(b - 1, leaf_count - 1)

    @pl.when(high_edge)
    def _():
        greet(b + 1, 0)

    for load in loads[3:]:
        load.start()

    @pl.when(p == 0)
    def _():
        value_win[0:cell_pairs] = jnp.zeros((cell_pairs, cols, 2 * leaf_size), BF16)
        coef_win[0:coef_pairs] = jnp.zeros((coef_pairs, cols, 2 * rank), BF16)

    @pl.when(p == last)
    def _():
        value_win[2 * cell_pairs : 3 * cell_pairs] = jnp.zeros(
            (cell_pairs, cols, 2 * leaf_size), BF16
        )
        coef_win[2 * coef_pairs : 3 * coef_pairs] = jnp.zeros((coef_pairs, cols, 2 * rank), BF16)

    val_load.wait()
    cells = val[...].reshape(cols, leaves * leaf_size)
    for t in range(cell_pairs):
        value_win[cell_pairs + t] = cells[:, 2 * t * leaf_size : 2 * (t + 1) * leaf_size]

    greeted = leaf_count - 1 + branch_count - 1
    greeted += low_edge.astype(jnp.int32) + high_edge.astype(jnp.int32)
    pl.semaphore_wait(barrier, greeted)

    def halo(window, size, kind, way):
        place = 0 if way == 0 else 2 * size
        other = p + 1 if way == 0 else p - 1
        return pltpu.make_async_remote_copy(
            src_ref=window.at[pl.ds(size, size)],
            dst_ref=window.at[pl.ds(place, size)],
            send_sem=halo_send.at[2 * kind + way],
            recv_sem=halo_recv.at[2 * kind + way],
            device_id=(other // leaf_count, lax.rem(other, leaf_count)),
            device_id_type=MESH,
        )

    def for_ways(act):
        @pl.when(p < last)
        def _():
            act(0)

        @pl.when(p > 0)
        def _():
            act(1)

    def value_halo(way):
        return halo(value_win, cell_pairs, 0, way)

    def coef_halo(way):
        return halo(coef_win, coef_pairs, 1, way)

    for_ways(lambda way: value_halo(way).start())
    basis_load.wait()
    level = []
    for t in range(cell_pairs):
        pair = cells[:, 2 * t * leaf_size : 2 * (t + 1) * leaf_size]
        level.append(dot(pair[:, :leaf_size], basis[2 * t]).astype(BF16))
        level.append(dot(pair[:, leaf_size:], basis[2 * t + 1]).astype(BF16))
    trans_load.wait()
    for step in range(LOG_LEAF):
        above = []
        for t in range(leaves >> step + 1):
            low = starts[step] + 2 * t
            pair = side_by_side(level[2 * t : 2 * t + 2])
            coef_win[coef_pairs + low // 2] = pair
            mats = trans[low : low + 2].reshape(2 * rank, rank)
            above.append(dot(pair, mats).astype(BF16))
        level = above
    leaf_roots[j] = dense(level[0])

    def leaf_copy(d, slot):
        return pltpu.make_async_remote_copy(
            src_ref=leaf_roots.at[slot],
            dst_ref=leaf_roots.at[slot],
            send_sem=leaf_send.at[d - 1],
            recv_sem=leaf_recv.at[d - 1],
            device_id=(b, lax.rem(j + d, leaf_count)),
            device_id_type=MESH,
        )

    for d in range(1, leaf_count):
        leaf_copy(d, j).start()

    for_ways(lambda way: coef_halo(way).start())

    first = lax.broadcasted_iota(jnp.int32, (rank, cols), 1) < rhs_count

    def pick(both):
        return jnp.where(first, both[:rank], both[rank:])

    def spread(pair, table, place):
        half = pair.shape[1] // 2
        turned = jnp.concatenate([pair[:, half:], pair[:, :half]], axis=1)
        table[place] = jnp.concatenate([pair[:, :half], turned[:, half:]], axis=1)
        table[place + 1] = jnp.concatenate([turned[:, :half], pair[:, half:]], axis=1)

    def spread_values(side):
        for t in range(0, leaves, 2):
            spread(value_win[side * cell_pairs + t // 2], value_table, side * leaves + t)

    def spread_coefs(side):
        for step in range(LOG_LEAF):
            count = leaves >> step
            for t in range(0, count, 2):
                pair = coef_win[side * coef_pairs + (starts[step] + t) // 2]
                spread(pair, coef_table, 3 * starts[step] + side * count + t)

    spread_values(1)
    spread_coefs(1)

    def listed(matrices, row, count, window, source):
        wide = side_by_side(
            [matrices[:, row, m].reshape(operators * rank, rank) for m in range(count)]
        )
        picked = []
        for m in range(0, count, 2):
            half = window.shape[2] // 2
            left, right = window[source(m)], window[source(m + 1)]
            picked.append(jnp.concatenate([left[:, :half], right[:, half:]], axis=1))
        return pick(dot_nt(wide, jnp.concatenate(picked, axis=1)))

    ut_load.wait()
    offsets = [2 * leaf_count - 2 * (leaf_count >> step) for step in range(depth + 1)]
    above = [up_trans[offsets[depth] - 2], up_trans[offsets[depth] - 1]]
    for step in range(depth - 2, -1, -1):
        below = []
        for t, path in enumerate(above):
            low = offsets[step] + 2 * t
            mats = up_trans[low : low + 2].reshape(2 * rank, rank)
            both = dot(mats, path).astype(BF16)
            below += [both[:rank], both[rank:]]
        above = below
    for t, path in enumerate(above):
        paths[t] = path

    for_ways(lambda way: value_halo(1 - way).wait_recv())
    spread_values(0)
    spread_values(2)
    ni_load.wait()

    def near_step(t, carry):
        near_part[t] = listed(near, t, near_blocks, value_table, lambda m: near_index[t, m])
        return carry

    for i, (low, high) in enumerate(chunks):
        for load in near_loads[i * operators : (i + 1) * operators]:
            load.wait()
        for t in range(low, high):
            near_step(t, 0)

    for_ways(lambda way: coef_halo(1 - way).wait_recv())
    spread_coefs(0)
    spread_coefs(2)
    ci_load.wait()

    def couple_row(row, begin):
        return listed(
            couple, row, blocks, coef_table, lambda m: 3 * begin + coupling_index[row, m]
        )

    for load in couple_loads[:operators]:
        load.wait()
    ready = {}
    for step in range(1, LOG_LEAF):
        for row in range(starts[step], starts[step] + (leaves >> step)):
            ready[row] = couple_row(row, starts[step])

    for d in range(1, leaf_count):
        leaf_copy(d, lax.rem(j + leaf_count - d, leaf_count)).wait_recv()
    level = [undense(leaf_roots[m]) for m in range(leaf_count)]
    root = dot(side_by_side(level), paths[...].reshape(leaf_count * rank, rank))
    own_root[...] = dense(root.astype(BF16))

    def branch_copy(d):
        return pltpu.make_async_remote_copy(
            src_ref=own_root,
            dst_ref=roots.at[branch_count - 1 - d],
            send_sem=branch_send.at[d - 1],
            recv_sem=branch_recv.at[d - 1],
            device_id=(lax.rem(b + d, branch_count), j),
            device_id_type=MESH,
        )

    for d in range(1, branch_count):
        branch_copy(d).start()

    for step in range(depth - 1):
        above = []
        for t in range(leaf_count >> step + 1):
            low = offsets[step] + 2 * t
            pair = side_by_side(level[2 * t : 2 * t + 2])
            mats = up_trans[low : low + 2].reshape(2 * rank, rank)
            coef = dot(pair, mats).astype(BF16)
            upper[offsets[step + 1] - leaf_count + t] = coef
            above.append(coef)
        level = above

    uc_load.wait()
    top_load.wait()
    for load in couple_loads[operators:]:
        load.wait()
    sides = []
    for step in range(depth):
        own = jnp.right_shift(j, step)
        mats = up_couple[:, offsets[step] + own].reshape(operators * rank, rank)
        sibling = jnp.bitwise_xor(own, 1)
        if step == 0:
            sibling = undense(leaf_roots[sibling])
        else:
            sibling = upper[offsets[step] - leaf_count + sibling]
        sides.append(pick(dot_nt(mats, sibling)))

    rest = sides[depth - 1].astype(BF16)
    for step in range(depth - 2, -1, -1):
        mat = up_trans[offsets[step] + jnp.right_shift(j, step)]
        rest = (sides[step] + dot(mat, rest)).astype(BF16)
    targets = [jnp.concatenate([rest, paths[j]], axis=1)]
    blank = jnp.zeros((2 * rank, rank), F32)

    known, from_top = [], []
    for step in range(LOG_LEAF - 1, -1, -1):
        below = []
        for t, parent in enumerate(targets):
            low = starts[step] + 2 * t
            mats = trans[low : low + 2].reshape(2 * rank, rank)
            if step == 0:
                pair = [couple_row(low + u, starts[step]) for u in range(2)]
            else:
                pair = [ready[low + u] for u in range(2)]
            both = jnp.concatenate([jnp.concatenate(pair, axis=0), blank], axis=1)
            both = (both + dot(mats, parent)).astype(BF16)
            children = [both[:rank], both[rank:]]
            below += children
            if step == 0:
                parts = []
                for u in range(2):
                    far = dot(basis[low + u], children[u])
                    parts.append(near_part[low + u] + far[:, :cols])
                    from_top.append(far[:, cols:].astype(BF16))
                known.append(jnp.concatenate(parts, axis=0).T)
        targets = below
    tops = side_by_side(
        [top[:, m].reshape(operators * rank, rank) for m in range(branch_count - 1)]
    )

    for d in range(1, branch_count):
        branch_copy(d).wait_recv()
    others = side_by_side([undense(roots[m]) for m in range(branch_count - 1)])
    crossed = dot_nt(others, tops)
    down = jnp.concatenate([crossed[:rhs_count, :rank], crossed[rhs_count:, rank:]], axis=0)
    down = down.astype(BF16)
    for t in range(0, leaves, 2):
        mats = jnp.concatenate(from_top[t : t + 2], axis=0)
        both = known[t // 2] + dot_nt(down, mats)
        out[:, :, t * leaf_size : (t + 2) * leaf_size] = both.reshape(
            operators, rhs_count, 2 * leaf_size
        )

    for d in range(1, leaf_count):
        leaf_copy(d, j).wait_send()
    for d in range(1, branch_count):
        branch_copy(d).wait_send()

    for_ways(lambda way: value_halo(way).wait_send())
    for_ways(lambda way: coef_halo(way).wait_send())


def solution(mesh):
    branch_count = mesh.shape["branch"]
    leaf_count = mesh.shape["leaf"]

    def per_device(
        values,
        leaf_basis,
        transfer,
        local_coupling,
        coupling_source,
        near_field,
        near_source,
        upper_transfer,
        upper_coupling,
        top_coupling,
    ):
        operators, rhs_count, width = values.shape
        cols = operators * rhs_count
        leaves, leaf_size, rank = leaf_basis.shape
        rows = transfer.shape[0]
        upper = upper_transfer.shape[1]
        any_spec = pl.BlockSpec(memory_space=pl.ANY)
        dma = pltpu.SemaphoreType.DMA

        def fixed(array):
            return pltpu.with_memory_space_constraint(array, pltpu.HBM)

        return pl.pallas_call(
            functools.partial(kernel, branch_count, leaf_count),
            out_shape=jax.ShapeDtypeStruct(values.shape, F32),
            in_specs=[any_spec] * 10,
            out_specs=pl.BlockSpec(memory_space=pltpu.VMEM),
            scratch_shapes=[
                pltpu.SMEM(coupling_source.shape, jnp.int32),
                pltpu.SMEM(near_source.shape, jnp.int32),
                pltpu.VMEM(values.shape, BF16),
                pltpu.VMEM(leaf_basis.shape, BF16),
                pltpu.VMEM(transfer.shape, BF16),
                pltpu.VMEM(local_coupling.shape, BF16),
                pltpu.VMEM(near_field.shape, BF16),
                pltpu.VMEM(upper_transfer.shape[1:], BF16),
                pltpu.VMEM((operators,) + upper_coupling.shape[2:], BF16),
                pltpu.VMEM((operators,) + top_coupling.shape[2:], BF16),
                pltpu.VMEM((3 * leaves // 2, cols, 2 * leaf_size), BF16),
                pltpu.VMEM((3 * rows // 2, cols, 2 * rank), BF16),
                pltpu.VMEM((3 * leaves, cols, 2 * leaf_size), BF16),
                pltpu.VMEM((3 * rows, cols, 2 * rank), BF16),
                pltpu.VMEM((leaf_count, rhs_count, operators * rank), BF16),
                pltpu.VMEM((leaf_count, rank, rank), BF16),
                pltpu.VMEM((upper - leaf_count, cols, rank), BF16),
                pltpu.VMEM((rhs_count, operators * rank), BF16),
                pltpu.VMEM((branch_count - 1, rhs_count, operators * rank), BF16),
                pltpu.VMEM((leaves, leaf_size, cols), F32),
                dma((8 + 4 * operators,)),
                dma((4,)),
                dma((4,)),
                dma((leaf_count - 1,)),
                dma((leaf_count - 1,)),
                dma((branch_count - 1,)),
                dma((branch_count - 1,)),
            ],
            compiler_params=pltpu.CompilerParams(
                collective_id=0, has_side_effects=True, vmem_limit_bytes=32 * 1024 * 1024
            ),
        )(
            fixed(values),
            fixed(leaf_basis),
            fixed(transfer),
            fixed(local_coupling),
            fixed(near_field),
            fixed(upper_transfer),
            fixed(upper_coupling),
            fixed(top_coupling),
            fixed(coupling_source),
            fixed(near_source),
        )

    in_specs = (
        P(None, None, ("branch", "leaf")),
        P(("branch", "leaf"), None, None),
        P(("branch", "leaf"), None, None),
        P(None, ("branch", "leaf"), None, None, None),
        P(("branch", "leaf"), None),
        P(None, ("branch", "leaf"), None, None, None),
        P(("branch", "leaf"), None),
        P("branch", None, None, None),
        P(None, "branch", None, None, None),
        P(None, "branch", None, None, None),
    )
    out_specs = P(None, None, ("branch", "leaf"))
    return jax.shard_map(
        per_device, mesh=mesh, in_specs=in_specs, out_specs=out_specs, check_vma=False
    )
```
